128 devices in a mesh: tmpl: 16 (over x, z_lo, core), seg: 8 (over z_hi, y).
Axes of the slice: x: 4, y: 4, z: 4 (z_hi: 2, z_lo: 2; z = z_hi * 2 + z_lo), core: 2. Of those that a mesh axis runs over, the one named last changes fastest.
Arguments:
- strain: float32 [2, 1024, 1024], P(None, 'seg'), may hold values from -6 to 6
- gate_start: int32 [2, 8, 2], P(None, 'seg'), may hold values from 0 to 131071
- gate_span: int32 [2, 8, 2], P(None, 'seg'), may hold values from 1 to 4096
- asd: float32 [1024, 1024], P(None, 'seg'), may hold values from 0.5 to 2
- bank: float32 [2, 32, 1024, 1024], P(None, None, 'tmpl', 'seg'), may hold values from -6 to 6
- assign: int32 [32], replicated, may hold values from 0 to 31, each once
Outputs:
- snr: float32 [2, 32, 1024, 1024], P(None, 'tmpl', None, 'seg')
The draws below stay inside these ranges and needn't reach their ends.
Inputs may be any that keep to these rules, and one draw needn't show every extreme that they name: `assign`: every template number appears exactly once.
All inputs are finite; a program needn't handle non-finite values.
Results may differ from the reference program's by a relative error of at most 0.0037.
Values may be sent and summed in bfloat16 or wider, within the bound.
No kernel may reach another device: no remote copies, remote signals or barrier semaphores. Data moves between devices by JAX's collectives and lax.ppermute only.
A program may use at most 128 MiB of HBM per device.

```python
import math
import jax
import jax.numpy as jnp
from jax import lax

N1 = 1024
N2 = 1024
NSAMP = 1048576
SEGS = 2
TEMPLATES = 32
BLOCKS = 8
BLOCK_LEN = 131072
GATES = 2
GATE_MAX = 4096


def with_ends(values, rng, smallest, largest):
    spot = [jax.random.randint(jax.random.fold_in(rng, axis), (), 0, length) for axis, length in enumerate(values.shape)]
    main_axis = values.shape.index(max(values.shape))
    next_to = spot[:main_axis] + [(spot[main_axis] + 1) % values.shape[main_axis]] + spot[main_axis + 1:]
    return values.at[tuple(spot)].set(smallest).at[tuple(next_to)].set(largest)


def block_levels(stream_key, shape, pieces, smallest, high):
    def one(dim, shards_of):
        draws = jax.random.uniform(jax.random.fold_in(jax.random.fold_in(stream_key, 6), dim), (shards_of,), jnp.float32, smallest / len(pieces), high / len(pieces))
        return jnp.repeat(jnp.exp(draws), shape[dim] // shards_of).reshape((-1,) + (1,) * (len(shape) - dim - 1))

    level = one(*pieces[0])
    for cut in pieces[1:]:
        level = level * one(*cut)
    return level


def bell_draw(stream_key, dims, width, bound, split=(), held_as=jnp.bfloat16):
    gain = block_levels(stream_key, dims, split, -0.22, 0.18) if split else 1.0
    drawn = jax.random.normal(stream_key, dims, jnp.float32) * width * gain
    return jnp.minimum(jnp.maximum(drawn, -bound), bound).astype(held_as)


def setup_inputs(seed: int = 0) -> dict:
    streams_of = jax.random.split(jax.random.key(seed), 7)
    strain = bell_draw(streams_of[0], (SEGS, N2, N1), 1.0, 6.0, ((1, 8),), jnp.float32)
    gate_start = with_ends(jax.random.randint(streams_of[1], (SEGS, BLOCKS, GATES), 0, BLOCK_LEN), jax.random.fold_in(streams_of[1], 1), 0, BLOCK_LEN - 1).astype(jnp.int32)
    gate_span = with_ends(jax.random.randint(streams_of[2], (SEGS, BLOCKS, GATES), 1, GATE_MAX + 1), jax.random.fold_in(streams_of[2], 1), 1, GATE_MAX).astype(jnp.int32)
    asd = jnp.clip(jnp.exp(math.log(2.0) - 1.3862944 * jax.random.uniform(streams_of[3], (N1, N2), jnp.float32) ** block_levels(streams_of[3], (N1, N2), ((1, 8),), -0.2, 0.2)), 0.5, 2.0)
    bank = bell_draw(streams_of[4], (2, TEMPLATES, N1, N2), 1.0, 6.0, ((2, 16), (3, 8)), jnp.float32)
    assign = jax.random.permutation(streams_of[5], TEMPLATES).astype(jnp.int32)
    return dict(strain=strain, gate_start=gate_start, gate_span=gate_span, asd=asd, bank=bank, assign=assign)


def phase_table(rows, cols, count):
    product = rows[:, None] * cols[None, :] % count
    return 2.0 * math.pi / count * product.astype(jnp.float32)

def rounded(value):
    return lax.optimization_barrier(value.astype(jnp.bfloat16)).astype(jnp.float32)

def reference(strain, gate_start, gate_span, asd, bank, assign):
    sample = jnp.arange(NSAMP, dtype=jnp.int32)
    offset = sample % BLOCK_LEN
    owner = sample // BLOCK_LEN
    gate_keep = jnp.ones((SEGS, NSAMP), jnp.float32)
    for gate_index in range(GATES):
        gate_first = gate_start[:, owner, gate_index]
        gate_len = gate_span[:, owner, gate_index]
        inside = (offset[None, :] >= gate_first) & (offset[None, :] < gate_first + gate_len)
        gate_keep = jnp.where(inside, jnp.float32(0.0), gate_keep)
    gated = strain.reshape(SEGS, NSAMP) * gate_keep
    spectrum = jnp.fft.fft(gated, axis=1).reshape(SEGS, N1, N2)
    spec_re = jnp.real(spectrum)
    spec_im = jnp.imag(spectrum)
    weight = 1.0 / (asd * asd)
    chosen = jnp.take(bank, assign, axis=0 + 1)
    sigma2 = lax.optimization_barrier(jnp.sum((chosen[0] * chosen[0] + chosen[1] * chosen[1]) * weight[None], axis=(1, 2)))
    fast_idx = jnp.arange(N1, dtype=jnp.int32)
    slow_idx = jnp.arange(N2, dtype=jnp.int32)
    fast_phase = phase_table(fast_idx, fast_idx, N1)
    fast_cos = rounded(jnp.cos(fast_phase))
    fast_sin = rounded(jnp.sin(fast_phase))
    slow_phase = phase_table(slow_idx, slow_idx, N2)
    slow_cos = rounded(jnp.cos(slow_phase))
    slow_sin = rounded(jnp.sin(slow_phase))
    twist = phase_table(fast_idx, slow_idx, NSAMP)
    twist_cos = jnp.cos(twist)
    twist_sin = jnp.sin(twist)
    precise = lax.Precision.HIGHEST

    def per_template(template_item):
        bank_re, bank_im, norm_value = template_item
        filt_re = rounded((spec_re * bank_re + spec_im * bank_im) * weight)
        filt_im = rounded((spec_im * bank_re - spec_re * bank_im) * weight)
        sum_re = jnp.einsum('ak,skb->sab', fast_cos, filt_re, precision=precise) - jnp.einsum('ak,skb->sab', fast_sin, filt_im, precision=precise)
        sum_im = jnp.einsum('ak,skb->sab', fast_sin, filt_re, precision=precise) + jnp.einsum('ak,skb->sab', fast_cos, filt_im, precision=precise)
        inner_re = rounded(sum_re * twist_cos - sum_im * twist_sin)
        inner_im = rounded(sum_re * twist_sin + sum_im * twist_cos)
        series_re = jnp.einsum('bk,sak->sba', slow_cos, inner_re, precision=precise) - jnp.einsum('bk,sak->sba', slow_sin, inner_im, precision=precise)
        series_im = jnp.einsum('bk,sak->sba', slow_sin, inner_re, precision=precise) + jnp.einsum('bk,sak->sba', slow_cos, inner_im, precision=precise)
        return jnp.sqrt(series_re * series_re + series_im * series_im) / jnp.sqrt(NSAMP * norm_value)
    snr = lax.map(per_template, (chosen[0], chosen[1], sigma2))
    return jnp.transpose(snr, (1, 0, 2, 3))
```

```python
import functools
import math

import jax
import jax.numpy as jnp
import numpy as np
from jax import lax
from jax.experimental import pallas as pl
from jax.experimental.pallas import tpu as pltpu
from jax.sharding import PartitionSpec as P

BF = jnp.bfloat16
F32 = jnp.float32
NSAMP = 1048576
VMEM = pl.BlockSpec(memory_space=pltpu.VMEM)
SMEM = pl.BlockSpec(memory_space=pltpu.SMEM)
ANY = pl.BlockSpec(memory_space=pl.ANY)
MIB = 1 << 20


def phases(product, count):
    angle = 2.0 * math.pi / count * (product % count).astype(np.float64)
    return np.cos(angle), np.sin(angle)


def split_hi_lo(table):
    table = table.astype(np.float32)
    hi = table.astype(jnp.bfloat16)
    lo = (table - hi.astype(np.float32)).astype(jnp.bfloat16)
    return hi, lo


@functools.cache
def tables():
    q = np.arange(256)
    select = np.zeros((2, 256, 128), np.float32)
    for core in range(2):
        for seg in range(2):
            for j in range(64):
                select[core, seg * 128 + core * 64 + j, seg * 64 + (j % 4) * 16 + j // 4] = 1.0
    order = np.zeros((128, 128), np.float32)
    for m in range(128):
        order[(m % 4) * 32 + m // 4, m] = 1.0
    first = []
    for r in range(4):
        c, s = phases((4 * q[:, None] + r) * q[None, :], 1024)
        first.append(np.stack([np.stack(split_hi_lo(c)), np.stack(split_hi_lo(-s))]))
    rows = np.array([4 * (i % 16) + i // 16 for i in range(64)])
    k2 = np.arange(1024)
    c, s = phases(rows[:, None] * k2[None, :], NSAMP)
    fine = np.stack([c, -s]).astype(np.float32)
    c, s = phases(64 * np.arange(16)[:, None] * k2[None, :], NSAMP)
    base = np.stack([c, -s]).astype(np.float32)
    n1 = np.array([128 * s + 64 * c + 4 * j for c in range(2) for s in range(8) for j in range(16)])
    second = []
    for r in range(4):
        c, s = phases(q[:, None] * (n1 + r)[None, :], 1024)
        (ch, cl), (sh, sl) = split_hi_lo(c), split_hi_lo(s)
        second.append(np.concatenate([ch, sh, cl, sl], axis=1))
    third = []
    for p in range(4):
        c, s = phases(q[:, None] * (4 * q[None, :] + p), 1024)
        c, s = c.astype(np.float32), s.astype(np.float32)
        third.append(np.stack([np.concatenate([c, -s], 1), np.concatenate([s, c], 1)]))
    c, s = phases(np.arange(1024)[:, None] * k2[None, :], NSAMP)
    back = np.stack([c, s]).astype(np.float32).reshape(2, 1024, 8, 128).transpose(2, 0, 1, 3)
    last = []
    for p in range(4):
        c, s = phases((4 * q[:, None] + p) * q[None, :], 1024)
        last.append(np.stack([c, s]).astype(np.float32))
    return dict(
        select=select.astype(jnp.bfloat16),
        order=order.astype(jnp.bfloat16),
        first=np.stack(first),
        fine=fine,
        base=base,
        second=np.stack(second),
        third=np.stack(third).astype(jnp.bfloat16),
        back=np.ascontiguousarray(back),
        last=np.stack(last).astype(jnp.bfloat16),
    )


def dot(a, b):
    return jnp.dot(a, b, preferred_element_type=F32)


def dot_nt(a, b):
    return lax.dot_general(a, b, (((1,), (1,)), ((), ())), preferred_element_type=F32)


def place():
    t = lax.axis_index("tmpl")
    return t // 4, (t // 2) % 2, t % 2


def gate_kernel(strain_ref, start_ref, span_ref, select_ref, order_ref, out_ref):
    _, _, core = place()
    pick = select_ref[core]
    order = order_ref[...]
    lane = lax.broadcasted_iota(jnp.int32, (128, 128), 1)
    row = lax.broadcasted_iota(jnp.int32, (128, 128), 0)
    for dest in range(8):
        cols = slice(128 * dest, 128 * dest + 128)
        sample = row * 1024 + lane + 128 * dest
        both = []
        for seg in range(2):
            value = strain_ref[seg, :, cols]
            for g in range(2):
                first = start_ref[seg, 0, g]
                inside = (sample >= first) & (sample < first + span_ref[seg, 0, g])
                value = jnp.where(inside, 0.0, value)
            both.append(value.astype(BF))
        picked = dot(jnp.concatenate(both, axis=1), pick).astype(BF)
        out_ref[dest] = dot(order, picked).astype(BF)


def pick_kernel(assign_ref, bank_ref, near_ref, cross_ref):
    x, z, core = place()

    def body(i, carry):
        rz, rx = i // 4, i % 4
        for rc in range(2):
            dest = ((x + rx) % 4) * 4 + (z + rz) % 2 * 2 + (core + rc) % 2
            for slot in range(2):
                chosen = assign_ref[2 * dest + slot]
                for part in range(2):
                    for p in range(4):
                        value = bank_ref[part, chosen, pl.ds(p, 16, stride=4), :].astype(BF)
                        if rc == 1:
                            cross_ref[rz, rx, slot, part, p] = value
                        else:
                            near_ref[rz, rx, slot, part, p] = value
        return carry

    lax.fori_loop(0, 8, body, 0)


def four_way(sign, parts):
    (ar, ai), (br, bi), (cr, ci), (dr, di) = parts
    sr, si = ar + cr, ai + ci
    tr, ti = ar - cr, ai - ci
    ur, ui = br + dr, bi + di
    vr, vi = br - dr, bi - di
    if sign > 0:
        wr, wi = -vi, vr
    else:
        wr, wi = vi, -vr
    return ((sr + ur, si + ui), (tr + wr, ti + wi), (sr - ur, si - ui), (tr - wr, ti - wi))


def first_kernel(cols_ref, table_ref, fine_ref, base_ref, out_ref, z_ref):
    _, _, core = place()
    group = 2 * lax.axis_index("seg") + core
    for r in range(4):
        piece = cols_ref[:, 32 * r : 32 * r + 32, :].reshape(256, 128)
        turned = piece.T
        for part in range(2):
            z_ref[r, part] = dot(turned, table_ref[r, part, 0]) + dot(turned, table_ref[r, part, 1])
    base_re = base_ref[0, pl.ds(group, 1), :]
    base_im = base_ref[1, pl.ds(group, 1), :]
    for r1 in range(4):
        rows = slice(16 * r1, 16 * r1 + 16)
        fr, fi = fine_ref[0, rows, :], fine_ref[1, rows, :]
        tr = fr * base_re - fi * base_im
        ti = fr * base_im + fi * base_re
        for seg in range(2):
            here = slice(64 * seg + 16 * r1, 64 * seg + 16 * r1 + 16)
            outs = four_way(-1, [(z_ref[r, 0, here, :], z_ref[r, 1, here, :]) for r in range(4)])
            for k, (re, im) in enumerate(outs):
                wr, wi = tr[:, 256 * k : 256 * k + 256], ti[:, 256 * k : 256 * k + 256]
                done = ((re * wr - im * wi).astype(BF), (re * wi + im * wr).astype(BF))
                for half in range(2):
                    for part in range(2):
                        out_ref[2 * k + half, part, seg, r1] = done[part][:, 128 * half : 128 * half + 128]


def filter_kernel(
    own_ref, other_ref, near_ref, cross_ref, side_ref, x1_ref, x2_ref, x3_ref, asd_ref, second_ref, third_ref, back_ref,
    out_ref,
    bank, twist, z_ref, spec, v_ref, sems,
):
    x, z, core = place()
    copies = []
    for rz in range(2):
        for rc in range(2):
            own = ((near_ref, cross_ref)[rc].at[0, 0]) if rz == 0 else side_ref.at[rc, 0]
            for dx, src in enumerate((own, x1_ref.at[rz, rc], x2_ref.at[rz, rc], x3_ref.at[rz, rc])):
                origin = ((x + 4 - dx) % 4) * 4 + (z + rz) % 2 * 2 + (core + rc) % 2
                copies.append(pltpu.make_async_copy(src, bank.at[origin], sems.at[len(copies)]))
    copies.append(pltpu.make_async_copy(back_ref.at[lax.axis_index("seg")], twist, sems.at[16]))
    for copy in copies:
        copy.start()
    low = core == 0
    for r in range(4):
        parts = []
        for part in range(2):
            lanes = []
            for seg in range(2):
                mine = own_ref[:, part, seg, r].reshape(128, 128)
                theirs = other_ref[:, part, seg, r].reshape(128, 128)
                lanes.append(
                    jnp.concatenate([jnp.where(low, mine, theirs), jnp.where(low, theirs, mine)], axis=0)
                )
            parts.append(jnp.concatenate(lanes, axis=1))
        re, im = parts
        table = second_ref[r]
        for part, stack in enumerate(([re, im], [im, -re])):
            right = jnp.concatenate(stack, axis=0)
            z_ref[r, part] = dot(table[:, :512], right) + dot(table[:, 512:], right)
    for i in range(8):
        rows = slice(32 * i, 32 * i + 32)
        outs = four_way(-1, [(z_ref[r, 0, rows, :], z_ref[r, 1, rows, :]) for r in range(4)])
        for k, (re, im) in enumerate(outs):
            here = slice(256 * k + 32 * i, 256 * k + 32 * i + 32)
            for seg in range(2):
                cols = slice(128 * seg, 128 * seg + 128)
                spec[0, seg, here, :] = re[:, cols]
                spec[1, seg, here, :] = im[:, cols]
    for copy in copies:
        copy.wait()
    norms = [jnp.zeros((8, 128), F32), jnp.zeros((8, 128), F32)]
    for p in range(4):
        asd = asd_ref[pl.ds(p, 256, stride=4), :]
        weight = 1.0 / (asd * asd)
        lanes_re, lanes_im = [], []
        heard = []
        for seg in range(2):
            heard.append([spec[part, seg, pl.ds(p, 256, stride=4), :] * weight for part in range(2)])
        for slot in range(2):
            hr = bank[:, slot, 0, p].reshape(256, 128).astype(F32)
            hi = bank[:, slot, 1, p].reshape(256, 128).astype(F32)
            power = (hr * hr + hi * hi) * weight
            norms[slot] = norms[slot] + power.reshape(32, 8, 128).sum(axis=0)
            for seg in range(2):
                sr, si = heard[seg]
                lanes_re.append((sr * hr + si * hi).astype(BF))
                lanes_im.append((si * hr - sr * hi).astype(BF))
        right = jnp.concatenate([jnp.concatenate(lanes_re, axis=1), jnp.concatenate(lanes_im, axis=1)], axis=0)
        v_ref[p, 0] = dot(third_ref[p, 0], right)
        v_ref[p, 1] = dot(third_ref[p, 1], right)
    for i in range(8):
        rows = slice(32 * i, 32 * i + 32)
        half, inside = i // 4, (i % 4) * 32
        for pair in range(4):
            slot, seg = pair // 2, pair % 2
            cols = slice(128 * pair, 128 * pair + 128)
            outs = four_way(1, [(v_ref[p, 0, rows, cols], v_ref[p, 1, rows, cols]) for p in range(4)])
            for k, (re, im) in enumerate(outs):
                wr = twist[0, 256 * k + 32 * i : 256 * k + 32 * i + 32, :]
                wi = twist[1, 256 * k + 32 * i : 256 * k + 32 * i + 32, :]
                at = (seg * 2 + slot) * 256 + inside
                out_ref[2 * k + half, at : at + 32, :] = (re * wr - im * wi).astype(BF)
                out_ref[2 * k + half, at + 128 : at + 160, :] = (re * wi + im * wr).astype(BF)
    row = lax.broadcasted_iota(jnp.int32, (16, 128), 0)
    tail = jnp.zeros((16, 128), F32)
    for slot in range(2):
        left = jnp.broadcast_to(norms[slot].sum(axis=0, keepdims=True), (16, 128))
        for piece in range(3):
            rounded = left.astype(BF).astype(F32)
            tail = jnp.where(row == 3 * slot + piece, rounded, tail)
            left = left - rounded
    for dest in range(8):
        out_ref[dest, 1024:1040, :] = tail.astype(BF)


def last_kernel(in_ref, table_ref, out_ref):
    total = jnp.zeros((16, 128), F32)
    for s in range(8):
        total = total + in_ref[s, 1024:1040, :].astype(F32)
    row = lax.broadcasted_iota(jnp.int32, (16, 128), 0)
    scales = []
    for slot in range(2):
        mine = (row >= 3 * slot) & (row < 3 * slot + 3)
        sigma2 = jnp.sum(jnp.where(mine, total, 0.0), axis=(0, 1), keepdims=True)
        scales.append(1.0 / jnp.sqrt(NSAMP * sigma2))
    for pair in range(4):
        seg, slot = pair // 2, pair % 2
        at = 256 * pair
        parts = []
        for r in range(4):
            both = jnp.concatenate([in_ref[2 * r, at : at + 256, :], in_ref[2 * r + 1, at : at + 256, :]], axis=1)
            both = both.astype(F32)
            parts.append((both[:128], both[128:]))
        outs = four_way(1, parts)
        for p, (re, im) in enumerate(outs):
            right = jnp.concatenate([re, im], axis=0)
            hi = right.astype(BF)
            lo = (right - hi.astype(F32)).astype(BF)
            cos = dot_nt(table_ref[p, 0], hi) + dot_nt(table_ref[p, 0], lo)
            sin = dot_nt(table_ref[p, 1], hi) + dot_nt(table_ref[p, 1], lo)
            sr = cos[:, :128] - sin[:, 128:]
            si = sin[:, :128] + cos[:, 128:]
            out_ref[seg, slot, pl.ds(p, 256, stride=4), :] = jnp.sqrt(sr * sr + si * si) * scales[slot]


def call(kernel, ins, outs, specs, flops, moved, scratch=(), limit=32):
    return pl.pallas_call(
        kernel,
        out_shape=outs,
        in_specs=specs,
        out_specs=jax.tree.map(lambda _: VMEM, outs),
        scratch_shapes=list(scratch),
        compiler_params=pltpu.CompilerParams(vmem_limit_bytes=limit * MIB),
        cost_estimate=pl.CostEstimate(flops=flops, bytes_accessed=moved, transcendentals=0),
    )(*ins)


def shape(*dims, dtype=BF):
    return jax.ShapeDtypeStruct(dims, dtype)


def per_device(strain, gate_start, gate_span, asd, bank, assign):
    const = {name: jnp.asarray(value) for name, value in tables().items()}
    swap_core = [(i, i ^ 1) for i in range(16)]
    swap_z = [(i, i ^ 2) for i in range(16)]

    gated = call(
        gate_kernel, (strain, gate_start, gate_span, const["select"], const["order"]), shape(8, 128, 128),
        [VMEM, SMEM, SMEM, VMEM, VMEM], 10**8, 2 * MIB,
    )
    columns = lax.all_to_all(gated, "seg", 0, 0)

    blk = (2, 2, 4, 16, 128)
    near, cross = call(
        pick_kernel, (assign, bank),
        (shape(2, 4, *blk), shape(2, 4, *blk)), [SMEM, VMEM], 10**8, 3 * MIB,
    )
    cross = lax.ppermute(cross, "tmpl", swap_core)
    side = lax.ppermute(jnp.stack([near[1], cross[1]]), "tmpl", swap_z)
    rounds = []
    for dx in range(1, 4):
        send = jnp.stack([jnp.stack([near[0, dx], cross[0, dx]]), side[:, dx]])
        hop = [(i, (i // 4 + dx) % 4 * 4 + i % 4) for i in range(16)]
        rounds.append(lax.ppermute(send, "tmpl", hop))

    turned = call(
        first_kernel, (columns, const["first"], const["fine"], const["base"]), shape(8, 2, 2, 4, 16, 128),
        [VMEM] * 4, 3 * 10**8, 4 * MIB, [pltpu.VMEM((4, 2, 128, 256), F32)],
    )
    own = lax.all_to_all(turned, "seg", 0, 0)
    other = lax.ppermute(own, "tmpl", swap_core)

    inner = call(
        filter_kernel,
        (own, other, near, cross, side, *rounds, asd, const["second"], const["third"], const["back"]),
        shape(8, 1040, 128),
        [VMEM] * 2 + [ANY] * 6 + [VMEM] * 3 + [ANY],
        3 * 10**9, 10 * MIB,
        [
            pltpu.VMEM((16, *blk), BF),
            pltpu.VMEM((2, 1024, 128), F32),
            pltpu.VMEM((4, 2, 256, 256), F32),
            pltpu.VMEM((2, 2, 1024, 128), F32),
            pltpu.VMEM((4, 2, 256, 512), F32),
            pltpu.SemaphoreType.DMA((17,)),
        ],
    )
    series = lax.all_to_all(inner, "seg", 0, 0)
    return call(
        last_kernel, (series, const["last"]), shape(2, 2, 1024, 128, dtype=F32), [VMEM] * 2, 3 * 10**9, 6 * MIB
    )


def solution(mesh):
    placed = (
        P(None, "seg", None),
        P(None, "seg", None),
        P(None, "seg", None),
        P(None, "seg"),
        P(None, None, "tmpl", "seg"),
        P(),
    )
    return jax.shard_map(
        per_device,
        mesh=mesh,
        in_specs=placed,
        out_specs=P(None, "tmpl", None, "seg"),
        check_vma=False,
    )
```

```python
import functools
import math

import jax
import jax.numpy as jnp
import numpy as np
from jax import lax
from jax.experimental import pallas as pl
from jax.experimental.pallas import tpu as pltpu
from jax.sharding import PartitionSpec as P

BF = jnp.bfloat16
F32 = jnp.float32
NSAMP = 1048576
VMEM = pl.BlockSpec(memory_space=pltpu.VMEM)
SMEM = pl.BlockSpec(memory_space=pltpu.SMEM)
ANY = pl.BlockSpec(memory_space=pl.ANY)
MIB = 1 << 20
OFFSETS = [(rz, rx) for rz in range(2) for rx in range(4)][1:]


def phases(product, count):
    angle = 2.0 * math.pi / count * (product % count).astype(np.float64)
    return np.cos(angle), np.sin(angle)


def split_hi_lo(table):
    table = table.astype(np.float32)
    hi = table.astype(jnp.bfloat16)
    lo = (table - hi.astype(np.float32)).astype(jnp.bfloat16)
    return hi, lo


@functools.cache
def tables():
    q = np.arange(256)
    first = []
    for r in range(4):
        c, s = phases((4 * q[:, None] + r) * q[None, :], 1024)
        first.append(np.stack([np.stack(split_hi_lo(c)), np.stack(split_hi_lo(-s))]))
    rows = np.array([4 * (i % 32) + i // 32 for i in range(128)])
    k2 = np.arange(1024)
    c, s = phases(rows[:, None] * k2[None, :], NSAMP)
    fine = np.stack([c, -s]).astype(np.float32)
    c, s = phases(128 * np.arange(8)[:, None] * k2[None, :], NSAMP)
    base = np.stack([c, -s]).astype(np.float32)
    second = []
    for r in range(4):
        c, s = phases(q[:, None] * (4 * q[None, :] + r), 1024)
        (ch, cl), (sh, sl) = split_hi_lo(c), split_hi_lo(s)
        second.append(np.concatenate([ch, sh, cl, sl], axis=1))
    third = []
    for p in range(4):
        c, s = phases(q[:, None] * (4 * q[None, :] + p), 1024)
        c, s = c.astype(np.float32), s.astype(np.float32)
        third.append(np.stack([np.concatenate([c, -s], 1), np.concatenate([s, c], 1)]))
    n1 = np.arange(1024)
    c, s = phases(n1[:, None] * np.arange(128)[None, :], NSAMP)
    back = np.stack([c, s]).astype(np.float32)
    c, s = phases(n1[:, None] * 128 * np.arange(128)[None, :], NSAMP)
    shift = np.stack([c, s]).astype(np.float32)
    last = []
    for p in range(4):
        c, s = phases((4 * q[:, None] + p) * q[None, :], 1024)
        last.append(np.stack([c, s]).astype(np.float32))
    return dict(
        first=np.stack(first),
        fine=fine,
        base=base,
        second=np.stack(second),
        third=np.stack(third).astype(jnp.bfloat16),
        back=back,
        shift=shift,
        last=np.stack(last).astype(jnp.bfloat16),
    )


def dot(a, b):
    return jnp.dot(a, b, preferred_element_type=F32)


def dot_nt(a, b):
    return lax.dot_general(a, b, (((1,), (1,)), ((), ())), preferred_element_type=F32)


def place():
    t = lax.axis_index("tmpl")
    return t // 4, (t // 2) % 2, t % 2


def gate_kernel(
    strain_ref, start_any, span_any, assign_any, bank_any, out_ref, near_ref, cross_ref,
    strain, bank_ref, start_ref, span_ref, assign_ref, sems,
):
    x, z, core = place()
    copies = [
        pltpu.make_async_copy(start_any, start_ref, sems.at[0]),
        pltpu.make_async_copy(span_any, span_ref, sems.at[1]),
        pltpu.make_async_copy(strain_ref.at[core], strain, sems.at[2]),
        pltpu.make_async_copy(assign_any, assign_ref, sems.at[3]),
        pltpu.make_async_copy(bank_any, bank_ref, sems.at[4]),
    ]
    for copy in copies:
        copy.start()
    row = lax.broadcasted_iota(jnp.int32, (128, 128), 0)
    lane = lax.broadcasted_iota(jnp.int32, (128, 128), 1)
    order = jnp.where(lane == row % 32 * 4 + row // 32, 1.0, 0.0).astype(BF)
    pick = jnp.where(row == lane % 32 * 4 + lane // 32, 1.0, 0.0).astype(BF)
    for copy in copies[:3]:
        copy.wait()
    blocks = []
    for dest in range(8):
        value = strain[:, 128 * dest : 128 * dest + 128]
        sample = row * 1024 + (lane + 128 * dest)
        for g in range(2):
            first = start_ref[core, 0, g]
            inside = (sample >= first) & (sample < first + span_ref[core, 0, g])
            value = jnp.where(inside, 0.0, value)
        blocks.append(value.astype(BF))
    picked = dot(jnp.concatenate(blocks, axis=0), pick).astype(BF)
    wide = jnp.concatenate([picked[128 * dest : 128 * dest + 128] for dest in range(8)], axis=1)
    ordered = dot(order, wide).astype(BF)
    for dest in range(8):
        out_ref[dest] = ordered[:, 128 * dest : 128 * dest + 128]

    for copy in copies[3:]:
        copy.wait()
    for i in range(16):
        rc, rz, rx = i // 8, i // 4 % 2, i % 4
        dest = ((x + rx) % 4) * 4 + (z + rz) % 2 * 2 + (core + rc) % 2
        for slot in range(2):
            chosen = assign_ref[2 * dest + slot]
            for part in range(2):
                for p in range(4):
                    value = bank_ref[part, chosen, pl.ds(p, 16, stride=4), :].astype(BF)
                    (near_ref, cross_ref)[rc][rz, rx, slot, part, p] = value


def prepare_kernel(asd_ref, back_ref, shift_ref, weight_ref, twist_ref):
    for p in range(4):
        asd = asd_ref[pl.ds(p, 256, stride=4), :]
        weight_ref[p] = 1.0 / (asd * asd)
    seg = lax.axis_index("seg")
    own = lax.broadcasted_iota(jnp.int32, (128, 128), 1) == seg
    for i in range(8):
        rows = slice(128 * i, 128 * i + 128)
        shift = [jnp.sum(jnp.where(own, shift_ref[part, rows, :], 0.0), axis=1, keepdims=True) for part in range(2)]
        re, im = back_ref[0, rows, :], back_ref[1, rows, :]
        twist_ref[0, rows, :] = re * shift[0] - im * shift[1]
        twist_ref[1, rows, :] = re * shift[1] + im * shift[0]


def pack_kernel(near_ref, cross_ref, *out_refs):
    for i, (rz, rx) in enumerate(OFFSETS):
        out_refs[i][0] = near_ref[rz, rx]
        out_refs[i][1] = cross_ref[rz, rx]


def four_way(sign, parts):
    (ar, ai), (br, bi), (cr, ci), (dr, di) = parts
    sr, si = ar + cr, ai + ci
    tr, ti = ar - cr, ai - ci
    ur, ui = br + dr, bi + di
    vr, vi = br - dr, bi - di
    if sign > 0:
        wr, wi = -vi, vr
    else:
        wr, wi = vi, -vr
    return ((sr + ur, si + ui), (tr + wr, ti + wi), (sr - ur, si - ui), (tr - wr, ti - wi))


def first_kernel(cols_ref, table_ref, fine_ref, base_ref, after_ref, also_ref, out_ref, z_ref):
    del after_ref, also_ref
    seg = lax.axis_index("seg")
    for r in range(4):
        turned = cols_ref[:, 32 * r : 32 * r + 32, :].reshape(256, 128).T
        for part in range(2):
            z_ref[r, part] = dot(turned, table_ref[r, part, 0]) + dot(turned, table_ref[r, part, 1])
    base_re = base_ref[0, pl.ds(seg, 1), :]
    base_im = base_ref[1, pl.ds(seg, 1), :]
    for i in range(8):
        rows = slice(16 * i, 16 * i + 16)
        at = slice(i % 2 * 16, i % 2 * 16 + 16)
        fr, fi = fine_ref[0, rows, :], fine_ref[1, rows, :]
        tr = fr * base_re - fi * base_im
        ti = fr * base_im + fi * base_re
        outs = four_way(-1, [(z_ref[r, 0, rows, :], z_ref[r, 1, rows, :]) for r in range(4)])
        for k, (re, im) in enumerate(outs):
            wr, wi = tr[:, 256 * k : 256 * k + 256], ti[:, 256 * k : 256 * k + 256]
            done = ((re * wr - im * wi).astype(BF), (re * wi + im * wr).astype(BF))
            for half in range(2):
                for part in range(2):
                    out_ref[2 * k + half, part, i // 2, at] = done[part][:, 128 * half : 128 * half + 128]


def second_kernel(own_ref, table_ref, after_ref, spec_ref, z_ref):
    del after_ref
    for r in range(4):
        re = own_ref[:, 0, r].reshape(256, 128)
        im = own_ref[:, 1, r].reshape(256, 128)
        right = jnp.concatenate([jnp.concatenate([re, im], axis=1), jnp.concatenate([im, -re], axis=1)], axis=0)
        z_ref[r] = dot(table_ref[r, :, :512], right) + dot(table_ref[r, :, 512:], right)
    for i in range(8):
        rows = slice(32 * i, 32 * i + 32)
        outs = four_way(-1, [(z_ref[r, rows, :128], z_ref[r, rows, 128:]) for r in range(4)])
        for k, parts in enumerate(outs):
            for part in range(2):
                spec_ref[part, 256 * k + 32 * i : 256 * k + 32 * i + 32, :] = parts[part]


def assemble_kernel(near_ref, cross_ref, *rest):
    moved_refs, bank, sems = rest[:7], rest[7], rest[8]
    x, z, core = place()
    copies = []
    for i, (rz, rx) in enumerate([(0, 0)] + OFFSETS):
        for rc in range(2):
            src = (near_ref, cross_ref)[rc].at[0, 0] if i == 0 else moved_refs[i - 1].at[rc]
            origin = ((x + 4 - rx) % 4) * 4 + (z + rz) % 2 * 2 + (core + rc) % 2
            copies.append(pltpu.make_async_copy(src, bank.at[origin], sems.at[len(copies)]))
    for copy in copies:
        copy.start()
    for copy in copies:
        copy.wait()


def filter_segment(spec, weight_ref, third_ref, twist, bank, out_ref, first_row, v_ref, norms):
    for p in range(4):
        weight = weight_ref[p]
        sr = spec[0, pl.ds(p, 256, stride=4), :] * weight
        si = spec[1, pl.ds(p, 256, stride=4), :] * weight
        lanes_re, lanes_im = [], []
        for slot in range(2):
            hr = bank[:, slot, 0, p].reshape(256, 128).astype(F32)
            hi = bank[:, slot, 1, p].reshape(256, 128).astype(F32)
            if norms is not None:
                power = (hr * hr + hi * hi) * weight
                norms[slot] = norms[slot] + power.reshape(32, 8, 128).sum(axis=0)
            lanes_re.append((sr * hr + si * hi).astype(BF))
            lanes_im.append((si * hr - sr * hi).astype(BF))
        right = jnp.concatenate([jnp.concatenate(lanes_re, axis=1), jnp.concatenate(lanes_im, axis=1)], axis=0)
        v_ref[p, 0] = dot(third_ref[p, 0], right)
        v_ref[p, 1] = dot(third_ref[p, 1], right)
    for i in range(8):
        rows = slice(32 * i, 32 * i + 32)
        half, inside = i // 4, (i % 4) * 32
        for slot in range(2):
            cols = slice(128 * slot, 128 * slot + 128)
            outs = four_way(1, [(v_ref[p, 0, rows, cols], v_ref[p, 1, rows, cols]) for p in range(4)])
            for k, (re, im) in enumerate(outs):
                wr = twist[0, 256 * k + 32 * i : 256 * k + 32 * i + 32, :]
                wi = twist[1, 256 * k + 32 * i : 256 * k + 32 * i + 32, :]
                at = first_row + slot * 256 + inside
                out_ref[2 * k + half, at : at + 32, :] = (re * wr - im * wi).astype(BF)
                out_ref[2 * k + half, at + 128 : at + 160, :] = (re * wi + im * wr).astype(BF)


def own_kernel(spec, weight_ref, third_ref, twist, bank, out_ref, v_ref):
    norms = [jnp.zeros((8, 128), F32), jnp.zeros((8, 128), F32)]
    filter_segment(spec, weight_ref, third_ref, twist, bank, out_ref, 0, v_ref, norms)
    row = lax.broadcasted_iota(jnp.int32, (16, 128), 0)
    tail = jnp.zeros((16, 128), F32)
    for slot in range(2):
        left = jnp.broadcast_to(norms[slot].sum(axis=0, keepdims=True), (16, 128))
        for piece in range(3):
            rounded = left.astype(BF).astype(F32)
            tail = jnp.where(row == 3 * slot + piece, rounded, tail)
            left = left - rounded
    for dest in range(8):
        out_ref[dest, 512:528, :] = tail.astype(BF)


def other_kernel(spec, weight_ref, third_ref, twist, bank, half_ref, out_ref, v_ref):
    out_ref[:, :528, :] = half_ref[...]
    filter_segment(spec, weight_ref, third_ref, twist, bank, out_ref, 528, v_ref, None)


def last_kernel(in_ref, table_ref, out_ref):
    total = jnp.zeros((16, 128), F32)
    for s in range(8):
        total = total + in_ref[s, 512:528, :].astype(F32)
    row = lax.broadcasted_iota(jnp.int32, (16, 128), 0)
    scales = []
    for slot in range(2):
        mine = (row >= 3 * slot) & (row < 3 * slot + 3)
        sigma2 = jnp.sum(jnp.where(mine, total, 0.0), axis=(0, 1), keepdims=True)
        scales.append(1.0 / jnp.sqrt(NSAMP * sigma2))
    _, _, core = place()
    for pair in range(4):
        other, slot = pair // 2, pair % 2
        seg = (core + other) % 2
        at = 528 * other + 256 * slot
        parts = []
        for r in range(4):
            both = jnp.concatenate([in_ref[2 * r, at : at + 256, :], in_ref[2 * r + 1, at : at + 256, :]], axis=1)
            both = both.astype(F32)
            parts.append((both[:128], both[128:]))
        outs = four_way(1, parts)
        for p, (re, im) in enumerate(outs):
            right = jnp.concatenate([re, im], axis=0)
            hi = right.astype(BF)
            lo = (right - hi.astype(F32)).astype(BF)
            cos = dot_nt(table_ref[p, 0], hi) + dot_nt(table_ref[p, 0], lo)
            sin = dot_nt(table_ref[p, 1], hi) + dot_nt(table_ref[p, 1], lo)
            sr = cos[:, :128] - sin[:, 128:]
            si = sin[:, :128] + cos[:, 128:]
            out_ref[seg, slot, pl.ds(p, 256, stride=4), :] = jnp.sqrt(sr * sr + si * si) * scales[slot]


def call(kernel, ins, outs, specs, flops, moved, scratch=(), limit=16):
    return pl.pallas_call(
        kernel,
        out_shape=outs,
        in_specs=specs,
        out_specs=jax.tree.map(lambda _: VMEM, outs),
        scratch_shapes=list(scratch),
        compiler_params=pltpu.CompilerParams(vmem_limit_bytes=limit * MIB),
        cost_estimate=pl.CostEstimate(flops=flops, bytes_accessed=moved, transcendentals=0),
    )(*ins)


def shape(*dims, dtype=BF):
    return jax.ShapeDtypeStruct(dims, dtype)


def per_device(strain, gate_start, gate_span, asd, bank, assign):
    const = {name: jnp.asarray(value) for name, value in tables().items()}
    swap_core = [(i, i ^ 1) for i in range(16)]

    blk = (2, 2, 4, 16, 128)
    gated, near, cross = call(
        gate_kernel, (strain, gate_start, gate_span, assign, bank),
        (shape(8, 128, 128), shape(2, 4, *blk), shape(2, 4, *blk)), [ANY] * 5, 10**8, 4 * MIB,
        [
            pltpu.VMEM((128, 1024), F32), pltpu.VMEM((2, 32, 64, 128), F32), pltpu.SMEM((2, 1, 2), jnp.int32),
            pltpu.SMEM((2, 1, 2), jnp.int32), pltpu.SMEM((32,), jnp.int32), pltpu.SemaphoreType.DMA((5,)),
        ],
        limit=63,
    )
    columns = lax.all_to_all(gated, "seg", 0, 0)

    cross = lax.ppermute(cross, "tmpl", swap_core)
    sends = call(pack_kernel, (near, cross), (shape(2, *blk),) * 7, [VMEM] * 2, 10**6, 2 * MIB)
    moved = []
    for (rz, rx), send in zip(OFFSETS, sends):
        hop = [(i, (i // 4 + rx) % 4 * 4 + i % 4 ^ 2 * rz) for i in range(16)]
        moved.append(lax.ppermute(send, "tmpl", hop))
    ordered = call(
        assemble_kernel, (near, cross, *moved), shape(16, *blk), [ANY] * 9, 1, 20 * MIB, [pltpu.SemaphoreType.DMA((16,))]
    )
    weight, twist = call(
        prepare_kernel, (asd, const["back"], const["shift"]),
        (shape(4, 256, 128, dtype=F32), shape(2, 1024, 128, dtype=F32)), [VMEM] * 3, 1, 40 * MIB,
    )
    turned = call(
        first_kernel, (columns, const["first"], const["fine"], const["base"], sends[0], weight),
        shape(8, 2, 4, 32, 128), [VMEM] * 4 + [ANY] * 2, 3 * 10**8, 4 * MIB, [pltpu.VMEM((4, 2, 128, 256), F32)],
    )
    own = lax.all_to_all(turned, "seg", 0, 0)
    spec = call(
        second_kernel, (own, const["second"], ordered), shape(2, 1024, 128, dtype=F32),
        [VMEM] * 2 + [ANY], 1, 1, [pltpu.VMEM((4, 256, 256), F32)],
    )
    other_spec = lax.ppermute(spec, "tmpl", swap_core)
    half = call(
        own_kernel,
        (spec, weight, const["third"], twist, ordered),
        shape(8, 528, 128), [VMEM] * 5, 2 * 10**9, 10 * MIB, [pltpu.VMEM((4, 2, 256, 256), F32)],
    )
    inner = call(
        other_kernel,
        (other_spec, weight, const["third"], twist, ordered, half),
        shape(8, 1040, 128), [VMEM] * 6, 2 * 10**9, 10 * MIB, [pltpu.VMEM((4, 2, 256, 256), F32)],
    )
    series = lax.all_to_all(inner, "seg", 0, 0)
    return call(
        last_kernel, (series, const["last"]), shape(2, 2, 1024, 128, dtype=F32), [VMEM] * 2, 3 * 10**9, 6 * MIB
    )


def solution(mesh):
    placed = (
        P(None, "seg", None),
        P(None, "seg", None),
        P(None, "seg", None),
        P(None, "seg"),
        P(None, None, "tmpl", "seg"),
        P(),
    )
    return jax.shard_map(
        per_device,
        mesh=mesh,
        in_specs=placed,
        out_specs=P(None, "tmpl", None, "seg"),
        check_vma=False,
    )
```

```python
import functools
import math

import jax
import jax.numpy as jnp
import numpy as np
from jax import lax
from jax.experimental import pallas as pl
from jax.experimental.pallas import tpu as pltpu
from jax.sharding import PartitionSpec as P

BF = jnp.bfloat16
F32 = jnp.float32
NSAMP = 1048576
VMEM = pl.BlockSpec(memory_space=pltpu.VMEM)
SMEM = pl.BlockSpec(memory_space=pltpu.SMEM)
ANY = pl.BlockSpec(memory_space=pl.ANY)
MIB = 1 << 20
OFFSETS = [(rz, rx) for rz in range(2) for rx in range(4)]


def phases(product, count):
    angle = 2.0 * math.pi / count * (product % count).astype(np.float64)
    return np.cos(angle), np.sin(angle)


def split_hi_lo(table):
    table = table.astype(np.float32)
    hi = table.astype(jnp.bfloat16)
    lo = (table - hi.astype(np.float32)).astype(jnp.bfloat16)
    return hi, lo


@functools.cache
def tables():
    q = np.arange(256)
    first = []
    for r in range(4):
        c, s = phases((4 * q[:, None] + r) * q[None, :], 1024)
        first.append(np.stack([np.stack(split_hi_lo(c)), np.stack(split_hi_lo(-s))]))
    k2 = np.arange(1024)
    rows = np.concatenate([4 * np.arange(32), 128 * np.arange(8), np.arange(8)])
    c, s = phases(rows[:, None] * k2[None, :], NSAMP)
    turn = np.stack([c, -s]).astype(np.float32)
    second = []
    for r in range(4):
        c, s = phases(q[:, None] * (4 * q[None, :] + r), 1024)
        (ch, cl), (sh, sl) = split_hi_lo(c), split_hi_lo(s)
        second.append(np.concatenate([ch, sh, cl, sl], axis=1))
    third = []
    for p in range(4):
        c, s = phases(q[:, None] * (4 * q[None, :] + p), 1024)
        c, s = c.astype(np.float32), s.astype(np.float32)
        third.append(np.stack([np.concatenate([c, -s], 1), np.concatenate([s, c], 1)]))
    n1 = np.arange(1024)
    c, s = phases(n1[:, None] * np.arange(128)[None, :], NSAMP)
    back = np.stack([c, s]).astype(np.float32)
    c, s = phases(n1[:, None] * 128 * np.arange(128)[None, :], NSAMP)
    shift = np.stack([c, s]).astype(np.float32)
    last = []
    for p in range(4):
        c, s = phases((4 * q[:, None] + p) * q[None, :], 1024)
        last.append(np.stack([c, s]).astype(np.float32))
    return dict(
        first=np.stack(first),
        turn=turn,
        second=np.stack(second),
        third=np.stack(third).astype(jnp.bfloat16),
        back=back,
        shift=shift,
        last=np.stack(last).astype(jnp.bfloat16),
    )


def dot(a, b):
    return jnp.dot(a, b, preferred_element_type=F32)


def dot_nt(a, b):
    return lax.dot_general(a, b, (((1,), (1,)), ((), ())), preferred_element_type=F32)


def place():
    t = lax.axis_index("tmpl")
    return t // 4, (t // 2) % 2, t % 2


def gate_kernel(
    strain_ref, start_any, span_any, assign_any, bank_any, asd_any, back_any, shift_any,
    out_ref, weight_ref, twist_ref, *rest
):
    pick_refs, rest = rest[:8], rest[8:]
    strain, bank_ref, start_ref, span_ref, assign_ref, asd_ref, back_ref, shift_ref, sems = rest
    x, z, core = place()
    copies = [
        pltpu.make_async_copy(start_any, start_ref, sems.at[0]),
        pltpu.make_async_copy(span_any, span_ref, sems.at[1]),
        pltpu.make_async_copy(strain_ref.at[core], strain, sems.at[2]),
        pltpu.make_async_copy(assign_any, assign_ref, sems.at[3]),
        pltpu.make_async_copy(bank_any, bank_ref, sems.at[4]),
        pltpu.make_async_copy(asd_any, asd_ref, sems.at[5]),
        pltpu.make_async_copy(back_any, back_ref, sems.at[6]),
        pltpu.make_async_copy(shift_any, shift_ref, sems.at[7]),
    ]
    for copy in copies:
        copy.start()
    row = lax.broadcasted_iota(jnp.int32, (128, 128), 0)
    lane = lax.broadcasted_iota(jnp.int32, (128, 128), 1)
    order = jnp.where(lane == row % 32 * 4 + row // 32, 1.0, 0.0).astype(BF)
    pick = jnp.where(row == lane % 32 * 4 + lane // 32, 1.0, 0.0).astype(BF)
    for copy in copies[:3]:
        copy.wait()
    blocks = []
    for dest in range(8):
        value = strain[:, 128 * dest : 128 * dest + 128]
        sample = row * 1024 + (lane + 128 * dest)
        for g in range(2):
            first = start_ref[core, 0, g]
            inside = (sample >= first) & (sample < first + span_ref[core, 0, g])
            value = jnp.where(inside, 0.0, value)
        blocks.append(value.astype(BF))
    picked = dot(jnp.concatenate(blocks, axis=0), pick).astype(BF)
    wide = jnp.concatenate([picked[128 * dest : 128 * dest + 128] for dest in range(8)], axis=1)
    ordered = dot(order, wide).astype(BF)
    for dest in range(8):
        out_ref[dest] = ordered[:, 128 * dest : 128 * dest + 128]

    for copy in copies[3:5]:
        copy.wait()
    for i in range(16):
        rz, rx, rc = i // 8, i // 2 % 4, i % 2
        dest = ((x + rx) % 4) * 4 + (z + rz) % 2 * 2 + (core + rc) % 2
        for slot in range(2):
            chosen = assign_ref[2 * dest + slot]
            for part in range(2):
                for p in range(4):
                    value = bank_ref[part, chosen, pl.ds(p, 16, stride=4), :].astype(BF)
                    pick_refs[i // 2][rc, slot, part, p] = value

    for copy in copies[5:]:
        copy.wait()
    for p in range(4):
        asd = asd_ref[pl.ds(p, 256, stride=4), :]
        weight_ref[p] = 1.0 / (asd * asd)
    own = lane == lax.axis_index("seg")
    for i in range(8):
        rows = slice(128 * i, 128 * i + 128)
        shift = [jnp.sum(jnp.where(own, shift_ref[part, rows, :], 0.0), axis=1, keepdims=True) for part in range(2)]
        re, im = back_ref[0, rows, :], back_ref[1, rows, :]
        twist_ref[0, rows, :] = re * shift[0] - im * shift[1]
        twist_ref[1, rows, :] = re * shift[1] + im * shift[0]


def pack_kernel(*refs):
    piece_refs, out_ref, token_ref, sems = refs[:8], *refs[8:]
    token_ref[...] = jnp.zeros_like(token_ref)
    copies = [pltpu.make_async_copy(piece_refs[i].at[1], out_ref.at[i], sems.at[i]) for i in range(8)]
    for copy in copies:
        copy.start()
    for copy in copies:
        copy.wait()


def four_way(sign, parts):
    (ar, ai), (br, bi), (cr, ci), (dr, di) = parts
    sr, si = ar + cr, ai + ci
    tr, ti = ar - cr, ai - ci
    ur, ui = br + dr, bi + di
    vr, vi = br - dr, bi - di
    if sign > 0:
        wr, wi = -vi, vr
    else:
        wr, wi = vi, -vr
    return ((sr + ur, si + ui), (tr + wr, ti + wi), (sr - ur, si - ui), (tr - wr, ti - wi))


def first_kernel(cols_ref, table_ref, turn_ref, after_ref, out_ref, z_ref):
    del after_ref
    for r in range(4):
        turned = cols_ref[:, 32 * r : 32 * r + 32, :].reshape(256, 128).T
        for part in range(2):
            z_ref[r, part] = dot(turned, table_ref[r, part, 0]) + dot(turned, table_ref[r, part, 1])
    seg = 32 + lax.axis_index("seg")
    seg_re, seg_im = turn_ref[0, pl.ds(seg, 1), :], turn_ref[1, pl.ds(seg, 1), :]
    for r1 in range(4):
        low_re, low_im = turn_ref[0, 40 + r1 : 41 + r1, :], turn_ref[1, 40 + r1 : 41 + r1, :]
        base_re = low_re * seg_re - low_im * seg_im
        base_im = low_re * seg_im + low_im * seg_re
        for i in range(2):
            at = slice(16 * i, 16 * i + 16)
            rows = slice(32 * r1 + 16 * i, 32 * r1 + 16 * i + 16)
            fr, fi = turn_ref[0, at, :], turn_ref[1, at, :]
            tr = fr * base_re - fi * base_im
            ti = fr * base_im + fi * base_re
            outs = four_way(-1, [(z_ref[r, 0, rows, :], z_ref[r, 1, rows, :]) for r in range(4)])
            for k, (re, im) in enumerate(outs):
                wr, wi = tr[:, 256 * k : 256 * k + 256], ti[:, 256 * k : 256 * k + 256]
                done = ((re * wr - im * wi).astype(BF), (re * wi + im * wr).astype(BF))
                for half in range(2):
                    for part in range(2):
                        out_ref[2 * k + half, part, r1, at] = done[part][:, 128 * half : 128 * half + 128]


def second_kernel(own_ref, table_ref, after_ref, spec_ref, z_ref):
    del after_ref
    for r in range(4):
        re = own_ref[:, 0, r].reshape(256, 128)
        im = own_ref[:, 1, r].reshape(256, 128)
        right = jnp.concatenate([jnp.concatenate([re, im], axis=1), jnp.concatenate([im, -re], axis=1)], axis=0)
        z_ref[r] = dot(table_ref[r, :, :512], right) + dot(table_ref[r, :, 512:], right)
    for i in range(8):
        rows = slice(32 * i, 32 * i + 32)
        outs = four_way(-1, [(z_ref[r, rows, :128], z_ref[r, rows, 128:]) for r in range(4)])
        for k, parts in enumerate(outs):
            for part in range(2):
                spec_ref[part, 256 * k + 32 * i : 256 * k + 32 * i + 32, :] = parts[part]


def assemble_kernel(*refs):
    piece_refs, cross_ref, bank, sems = refs[:8], refs[8], refs[9], refs[10]
    x, z, core = place()
    copies = []
    for i in range(8):
        for rc in range(2):
            src = piece_refs[i].at[0] if rc == 0 else cross_ref.at[i]
            origin = ((x + 4 - i % 4) % 4) * 4 + (z + i // 4) % 2 * 2 + (core + rc) % 2
            copies.append(pltpu.make_async_copy(src, bank.at[origin], sems.at[len(copies)]))
    for copy in copies:
        copy.start()
    for copy in copies:
        copy.wait()


def filter_segment(spec, weight_ref, third_ref, twist, bank, out_ref, first_row, v_ref, norms):
    for p in range(4):
        weight = weight_ref[p]
        sr = spec[0, pl.ds(p, 256, stride=4), :] * weight
        si = spec[1, pl.ds(p, 256, stride=4), :] * weight
        lanes_re, lanes_im = [], []
        for slot in range(2):
            hr = bank[:, slot, 0, p].reshape(256, 128).astype(F32)
            hi = bank[:, slot, 1, p].reshape(256, 128).astype(F32)
            if norms is not None:
                power = (hr * hr + hi * hi) * weight
                norms[slot] = norms[slot] + power.reshape(32, 8, 128).sum(axis=0)
            lanes_re.append((sr * hr + si * hi).astype(BF))
            lanes_im.append((si * hr - sr * hi).astype(BF))
        right = jnp.concatenate([jnp.concatenate(lanes_re, axis=1), jnp.concatenate(lanes_im, axis=1)], axis=0)
        v_ref[p, 0] = dot(third_ref[p, 0], right)
        v_ref[p, 1] = dot(third_ref[p, 1], right)
    for i in range(8):
        rows = slice(32 * i, 32 * i + 32)
        half, inside = i // 4, (i % 4) * 32
        for slot in range(2):
            cols = slice(128 * slot, 128 * slot + 128)
            outs = four_way(1, [(v_ref[p, 0, rows, cols], v_ref[p, 1, rows, cols]) for p in range(4)])
            for k, (re, im) in enumerate(outs):
                wr = twist[0, 256 * k + 32 * i : 256 * k + 32 * i + 32, :]
                wi = twist[1, 256 * k + 32 * i : 256 * k + 32 * i + 32, :]
                at = first_row + slot * 256 + inside
                out_ref[2 * k + half, at : at + 32, :] = (re * wr - im * wi).astype(BF)
                out_ref[2 * k + half, at + 128 : at + 160, :] = (re * wi + im * wr).astype(BF)


def own_kernel(spec, weight_ref, third_ref, twist, bank, out_ref, v_ref):
    norms = [jnp.zeros((8, 128), F32), jnp.zeros((8, 128), F32)]
    filter_segment(spec, weight_ref, third_ref, twist, bank, out_ref, 0, v_ref, norms)
    row = lax.broadcasted_iota(jnp.int32, (16, 128), 0)
    tail = jnp.zeros((16, 128), F32)
    for slot in range(2):
        left = jnp.broadcast_to(norms[slot].sum(axis=0, keepdims=True), (16, 128))
        for piece in range(3):
            rounded = left.astype(BF).astype(F32)
            tail = jnp.where(row == 3 * slot + piece, rounded, tail)
            left = left - rounded
    for dest in range(8):
        out_ref[dest, 512:528, :] = tail.astype(BF)


def other_kernel(spec, weight_ref, third_ref, twist, bank, half_ref, out_ref, v_ref):
    out_ref[:, :528, :] = half_ref[...]
    filter_segment(spec, weight_ref, third_ref, twist, bank, out_ref, 528, v_ref, None)


def last_kernel(in_ref, table_ref, out_ref):
    total = jnp.zeros((16, 128), F32)
    for s in range(8):
        total = total + in_ref[s, 512:528, :].astype(F32)
    row = lax.broadcasted_iota(jnp.int32, (16, 128), 0)
    scales = []
    for slot in range(2):
        mine = (row >= 3 * slot) & (row < 3 * slot + 3)
        sigma2 = jnp.sum(jnp.where(mine, total, 0.0), axis=(0, 1), keepdims=True)
        scales.append(1.0 / jnp.sqrt(NSAMP * sigma2))
    _, _, core = place()
    for pair in range(4):
        other, slot = pair // 2, pair % 2
        seg = (core + other) % 2
        at = 528 * other + 256 * slot
        parts = []
        for r in range(4):
            both = jnp.concatenate([in_ref[2 * r, at : at + 256, :], in_ref[2 * r + 1, at : at + 256, :]], axis=1)
            both = both.astype(F32)
            parts.append((both[:128], both[128:]))
        outs = four_way(1, parts)
        for p, (re, im) in enumerate(outs):
            right = jnp.concatenate([re, im], axis=0)
            hi = right.astype(BF)
            lo = (right - hi.astype(F32)).astype(BF)
            cos = dot_nt(table_ref[p, 0], hi) + dot_nt(table_ref[p, 0], lo)
            sin = dot_nt(table_ref[p, 1], hi) + dot_nt(table_ref[p, 1], lo)
            sr = cos[:, :128] - sin[:, 128:]
            si = sin[:, :128] + cos[:, 128:]
            out_ref[seg, slot, pl.ds(p, 256, stride=4), :] = jnp.sqrt(sr * sr + si * si) * scales[slot]


def call(kernel, ins, outs, specs, flops, moved, scratch=(), limit=16, space=VMEM):
    return pl.pallas_call(
        kernel,
        out_shape=outs,
        in_specs=specs,
        out_specs=space if isinstance(space, tuple) else jax.tree.map(lambda _: space, outs),
        scratch_shapes=list(scratch),
        compiler_params=pltpu.CompilerParams(vmem_limit_bytes=limit * MIB),
        cost_estimate=pl.CostEstimate(flops=flops, bytes_accessed=moved, transcendentals=0),
    )(*ins)


def shape(*dims, dtype=BF):
    return jax.ShapeDtypeStruct(dims, dtype)


def per_device(strain, gate_start, gate_span, asd, bank, assign):
    const = {name: jnp.asarray(value) for name, value in tables().items()}
    swap_core = [(i, i ^ 1) for i in range(16)]

    blk = (2, 2, 4, 16, 128)
    gated, weight, twist, *picked = call(
        gate_kernel, (strain, gate_start, gate_span, assign, bank, asd, const["back"], const["shift"]),
        (
            shape(8, 128, 128), shape(4, 256, 128, dtype=F32), shape(2, 1024, 128, dtype=F32),
            *[shape(2, *blk)] * 8,
        ),
        [ANY] * 8, 10**8, 4 * MIB,
        [
            pltpu.VMEM((128, 1024), F32), pltpu.VMEM((2, 32, 64, 128), F32), pltpu.SMEM((2, 1, 2), jnp.int32),
            pltpu.SMEM((2, 1, 2), jnp.int32), pltpu.SMEM((32,), jnp.int32), pltpu.VMEM((1024, 128), F32),
            pltpu.VMEM((2, 1024, 128), F32), pltpu.VMEM((2, 1024, 128), F32), pltpu.SemaphoreType.DMA((8,)),
        ],
        limit=63,
    )
    columns = lax.all_to_all(gated, "seg", 0, 0)

    pieces = picked[:1]
    for (rz, rx), send in zip(OFFSETS[1:], picked[1:]):
        hop = [(i, (i // 4 + rx) % 4 * 4 + i % 4 ^ 2 * rz) for i in range(16)]
        pieces.append(lax.ppermute(send, "tmpl", hop))
    cross, token = call(
        pack_kernel, pieces, (shape(8, *blk), shape(8, 128, dtype=F32)), [ANY] * 8, 1, 10 * MIB,
        [pltpu.SemaphoreType.DMA((8,))], limit=8, space=(ANY, VMEM),
    )
    crossed = lax.ppermute(cross, "tmpl", swap_core)
    ordered = call(
        assemble_kernel, (*pieces, crossed), shape(16, *blk), [ANY] * 9, 1, 10 * MIB, [pltpu.SemaphoreType.DMA((16,))],
        limit=8,
    )
    turned = call(
        first_kernel, (columns, const["first"], const["turn"], token),
        shape(8, 2, 4, 32, 128), [VMEM] * 3 + [ANY], 3 * 10**8, 4 * MIB, [pltpu.VMEM((4, 2, 128, 256), F32)],
    )
    own = lax.all_to_all(turned, "seg", 0, 0)
    spec = call(
        second_kernel, (own, const["second"], ordered), shape(2, 1024, 128, dtype=F32),
        [VMEM] * 2 + [ANY], 1, 1, [pltpu.VMEM((4, 256, 256), F32)],
    )
    other_spec = lax.ppermute(spec, "tmpl", swap_core)
    half = call(
        own_kernel,
        (spec, weight, const["third"], twist, ordered),
        shape(8, 528, 128), [VMEM] * 5, 2 * 10**9, 10 * MIB, [pltpu.VMEM((4, 2, 256, 256), F32)],
    )
    inner = call(
        other_kernel,
        (other_spec, weight, const["third"], twist, ordered, half),
        shape(8, 1040, 128), [VMEM] * 6, 2 * 10**9, 10 * MIB, [pltpu.VMEM((4, 2, 256, 256), F32)],
    )
    series = lax.all_to_all(inner, "seg", 0, 0)
    return call(
        last_kernel, (series, const["last"]), shape(2, 2, 1024, 128, dtype=F32), [VMEM] * 2, 3 * 10**9, 6 * MIB
    )


def solution(mesh):
    placed = (
        P(None, "seg", None),
        P(None, "seg", None),
        P(None, "seg", None),
        P(None, "seg"),
        P(None, None, "tmpl", "seg"),
        P(),
    )
    return jax.shard_map(
        per_device,
        mesh=mesh,
        in_specs=placed,
        out_specs=P(None, "tmpl", None, "seg"),
        check_vma=False,
    )
```

```python
import functools
import math

import jax
import jax.numpy as jnp
import numpy as np
from jax import lax
from jax.experimental import pallas as pl
from jax.experimental.pallas import tpu as pltpu
from jax.sharding import PartitionSpec as P

BF = jnp.bfloat16
F32 = jnp.float32
NSAMP = 1048576
VMEM = pl.BlockSpec(memory_space=pltpu.VMEM)
SMEM = pl.BlockSpec(memory_space=pltpu.SMEM)
ANY = pl.BlockSpec(memory_space=pl.ANY)
MIB = 1 << 20
OFFSETS = [(0, 0), (1, 0), (1, 2), (1, 1), (1, 3), (0, 2), (0, 1), (0, 3)]


def phases(product, count):
    angle = 2.0 * math.pi / count * (product % count).astype(np.float64)
    return np.cos(angle), np.sin(angle)


def split_hi_lo(table):
    table = table.astype(np.float32)
    hi = table.astype(jnp.bfloat16)
    lo = (table - hi.astype(np.float32)).astype(jnp.bfloat16)
    return hi, lo


@functools.cache
def tables():
    q = np.arange(256)
    first = []
    for r in range(4):
        c, s = phases((4 * q[:, None] + r) * q[None, :], 1024)
        first.append(np.stack([np.stack(split_hi_lo(c)), np.stack(split_hi_lo(-s))]))
    k2 = np.arange(1024)
    rows = np.concatenate([4 * np.arange(32), 128 * np.arange(8), np.arange(8)])
    c, s = phases(rows[:, None] * k2[None, :], NSAMP)
    turn = np.stack([c, -s]).astype(np.float32)
    second = []
    for r in range(4):
        c, s = phases(q[:, None] * (4 * q[None, :] + r), 1024)
        (ch, cl), (sh, sl) = split_hi_lo(c), split_hi_lo(s)
        second.append(np.concatenate([ch, sh, cl, sl], axis=1))
    third = []
    for p in range(4):
        c, s = phases(q[:, None] * (4 * q[None, :] + p), 1024)
        c, s = c.astype(np.float32), s.astype(np.float32)
        third.append(np.stack([np.concatenate([c, -s], 1), np.concatenate([s, c], 1)]))
    n1 = np.arange(1024)
    c, s = phases(n1[:, None] * np.arange(128)[None, :], NSAMP)
    back = np.stack([c, s]).astype(np.float32)
    c, s = phases(n1[:, None] * 128 * np.arange(128)[None, :], NSAMP)
    shift = np.stack([c, s]).astype(np.float32)
    last = []
    for p in range(4):
        c, s = phases((4 * q[:, None] + p) * q[None, :], 1024)
        last.append(np.stack([c, s]).astype(np.float32))
    return dict(
        first=np.stack(first),
        turn=turn,
        second=np.stack(second),
        third=np.stack(third).astype(jnp.bfloat16),
        back=back,
        shift=shift,
        last=np.stack(last).astype(jnp.bfloat16),
    )


def dot(a, b):
    return jnp.dot(a, b, preferred_element_type=F32)


def dot_nt(a, b):
    return lax.dot_general(a, b, (((1,), (1,)), ((), ())), preferred_element_type=F32)


def place():
    t = lax.axis_index("tmpl")
    return t // 4, (t // 2) % 2, t % 2


def gate_kernel(
    strain_ref, start_any, span_any, assign_any, bank_any, out_ref, *rest
):
    pick_refs, rest = rest[:8], rest[8:]
    strain, bank_ref, start_ref, span_ref, assign_ref, sems = rest
    x, z, core = place()
    copies = [
        pltpu.make_async_copy(start_any, start_ref, sems.at[0]),
        pltpu.make_async_copy(span_any, span_ref, sems.at[1]),
        pltpu.make_async_copy(strain_ref.at[core], strain, sems.at[2]),
        pltpu.make_async_copy(assign_any, assign_ref, sems.at[3]),
        pltpu.make_async_copy(bank_any, bank_ref, sems.at[4]),
    ]
    for copy in copies:
        copy.start()
    row = lax.broadcasted_iota(jnp.int32, (128, 128), 0)
    lane = lax.broadcasted_iota(jnp.int32, (128, 128), 1)
    order = jnp.where(lane == row % 32 * 4 + row // 32, 1.0, 0.0).astype(BF)
    pick = jnp.where(row == lane % 32 * 4 + lane // 32, 1.0, 0.0).astype(BF)
    for copy in copies[:3]:
        copy.wait()
    blocks = []
    for dest in range(8):
        value = strain[:, 128 * dest : 128 * dest + 128]
        sample = row * 1024 + (lane + 128 * dest)
        for g in range(2):
            first = start_ref[core, 0, g]
            inside = (sample >= first) & (sample < first + span_ref[core, 0, g])
            value = jnp.where(inside, 0.0, value)
        blocks.append(value.astype(BF))
    picked = dot(jnp.concatenate(blocks, axis=0), pick).astype(BF)
    wide = jnp.concatenate([picked[128 * dest : 128 * dest + 128] for dest in range(8)], axis=1)
    ordered = dot(order, wide).astype(BF)
    for dest in range(8):
        out_ref[dest] = ordered[:, 128 * dest : 128 * dest + 128]

    for copy in copies[3:5]:
        copy.wait()
    for i in range(16):
        (rz, rx), rc = OFFSETS[i // 2], i % 2
        dest = ((x + rx) % 4) * 4 + (z + rz) % 2 * 2 + (core + rc) % 2
        for slot in range(2):
            chosen = assign_ref[2 * dest + slot]
            for part in range(2):
                for p in range(4):
                    value = bank_ref[part, chosen, pl.ds(p, 16, stride=4), :].astype(BF)
                    pick_refs[i // 2][rc, slot, part, p] = value


def pack_kernel(*refs):
    piece_refs, out_ref, token_ref, sems = refs[:8], *refs[8:]
    token_ref[...] = jnp.zeros_like(token_ref)
    copies = [pltpu.make_async_copy(piece_refs[i].at[1], out_ref.at[i], sems.at[i]) for i in range(8)]
    for copy in copies:
        copy.start()
    for copy in copies:
        copy.wait()


def four_way(sign, parts):
    (ar, ai), (br, bi), (cr, ci), (dr, di) = parts
    sr, si = ar + cr, ai + ci
    tr, ti = ar - cr, ai - ci
    ur, ui = br + dr, bi + di
    vr, vi = br - dr, bi - di
    if sign > 0:
        wr, wi = -vi, vr
    else:
        wr, wi = vi, -vr
    return ((sr + ur, si + ui), (tr + wr, ti + wi), (sr - ur, si - ui), (tr - wr, ti - wi))


def first_kernel(cols_ref, table_any, turn_any, after_ref, out_ref, table_ref, turn_ref, z_ref, sems):
    del after_ref
    copies = [pltpu.make_async_copy(table_any.at[r], table_ref.at[r], sems.at[r]) for r in range(4)]
    copies += [pltpu.make_async_copy(turn_any, turn_ref, sems.at[4])]
    for copy in copies:
        copy.start()
    for r in range(4):
        copies[r].wait()
        turned = cols_ref[:, 32 * r : 32 * r + 32, :].reshape(256, 128).T
        for part in range(2):
            z_ref[r, part] = dot(turned, table_ref[r, part, 0]) + dot(turned, table_ref[r, part, 1])
    copies[4].wait()
    seg = 32 + lax.axis_index("seg")
    seg_re, seg_im = turn_ref[0, pl.ds(seg, 1), :], turn_ref[1, pl.ds(seg, 1), :]
    for r1 in range(4):
        low_re, low_im = turn_ref[0, 40 + r1 : 41 + r1, :], turn_ref[1, 40 + r1 : 41 + r1, :]
        base_re = low_re * seg_re - low_im * seg_im
        base_im = low_re * seg_im + low_im * seg_re
        for i in range(2):
            at = slice(16 * i, 16 * i + 16)
            rows = slice(32 * r1 + 16 * i, 32 * r1 + 16 * i + 16)
            fr, fi = turn_ref[0, at, :], turn_ref[1, at, :]
            tr = fr * base_re - fi * base_im
            ti = fr * base_im + fi * base_re
            outs = four_way(-1, [(z_ref[r, 0, rows, :], z_ref[r, 1, rows, :]) for r in range(4)])
            for k, (re, im) in enumerate(outs):
                wr, wi = tr[:, 256 * k : 256 * k + 256], ti[:, 256 * k : 256 * k + 256]
                done = ((re * wr - im * wi).astype(BF), (re * wi + im * wr).astype(BF))
                for half in range(2):
                    for part in range(2):
                        out_ref[2 * k + half, part, r1, at] = done[part][:, 128 * half : 128 * half + 128]


def second_kernel(own_ref, table_ref, after_ref, spec_ref, z_ref):
    del after_ref
    for r in range(4):
        re = own_ref[:, 0, r].reshape(256, 128)
        im = own_ref[:, 1, r].reshape(256, 128)
        right = jnp.concatenate([jnp.concatenate([re, im], axis=1), jnp.concatenate([im, -re], axis=1)], axis=0)
        z_ref[r] = dot(table_ref[r, :, :512], right) + dot(table_ref[r, :, 512:], right)
    for i in range(8):
        rows = slice(32 * i, 32 * i + 32)
        outs = four_way(-1, [(z_ref[r, rows, :128], z_ref[r, rows, 128:]) for r in range(4)])
        for k, parts in enumerate(outs):
            for part in range(2):
                spec_ref[part, 256 * k + 32 * i : 256 * k + 32 * i + 32, :] = parts[part]


def assemble_kernel(*refs):
    piece_refs, cross_ref, asd_any, back_any, shift_any = refs[:8], *refs[8:12]
    bank, weight_any, twist_any, token_ref, weight_ref, twist_ref, asd_ref, back_ref, shift_ref, sems = refs[12:]
    token_ref[...] = jnp.zeros_like(token_ref)
    x, z, core = place()
    copies = [
        pltpu.make_async_copy(asd_any, asd_ref, sems.at[16]),
        pltpu.make_async_copy(back_any, back_ref, sems.at[17]),
        pltpu.make_async_copy(shift_any, shift_ref, sems.at[18]),
    ]
    for i, (rz, rx) in enumerate(OFFSETS):
        for rc in range(2):
            src = piece_refs[i].at[0] if rc == 0 else cross_ref.at[i]
            origin = ((x + 4 - rx) % 4) * 4 + (z + rz) % 2 * 2 + (core + rc) % 2
            copies.append(pltpu.make_async_copy(src, bank.at[origin], sems.at[2 * i + rc]))
    for copy in copies:
        copy.start()
    copies[0].wait()
    for p in range(4):
        asd = asd_ref[pl.ds(p, 256, stride=4), :]
        weight_ref[p] = 1.0 / (asd * asd)
    copies[1].wait()
    copies[2].wait()
    own = lax.broadcasted_iota(jnp.int32, (128, 128), 1) == lax.axis_index("seg")
    for i in range(8):
        rows = slice(128 * i, 128 * i + 128)
        shift = [jnp.sum(jnp.where(own, shift_ref[part, rows, :], 0.0), axis=1, keepdims=True) for part in range(2)]
        re, im = back_ref[0, rows, :], back_ref[1, rows, :]
        twist_ref[0, rows, :] = re * shift[0] - im * shift[1]
        twist_ref[1, rows, :] = re * shift[1] + im * shift[0]
    outs = [
        pltpu.make_async_copy(weight_ref, weight_any, sems.at[19]),
        pltpu.make_async_copy(twist_ref, twist_any, sems.at[20]),
    ]
    for copy in outs:
        copy.start()
    for copy in copies[3:] + outs:
        copy.wait()


def filter_segment(spec, weight_ref, third_ref, twist, bank, out_ref, first_row, v_ref, norms):
    for p in range(4):
        weight = weight_ref[p]
        sr = spec[0, pl.ds(p, 256, stride=4), :] * weight
        si = spec[1, pl.ds(p, 256, stride=4), :] * weight
        lanes_re, lanes_im = [], []
        for slot in range(2):
            hr = bank[:, slot, 0, p].reshape(256, 128).astype(F32)
            hi = bank[:, slot, 1, p].reshape(256, 128).astype(F32)
            if norms is not None:
                power = (hr * hr + hi * hi) * weight
                norms[slot] = norms[slot] + power.reshape(32, 8, 128).sum(axis=0)
            lanes_re.append((sr * hr + si * hi).astype(BF))
            lanes_im.append((si * hr - sr * hi).astype(BF))
        right = jnp.concatenate([jnp.concatenate(lanes_re, axis=1), jnp.concatenate(lanes_im, axis=1)], axis=0)
        v_ref[p, 0] = dot(third_ref[p, 0], right)
        v_ref[p, 1] = dot(third_ref[p, 1], right)
    for i in range(8):
        rows = slice(32 * i, 32 * i + 32)
        half, inside = i // 4, (i % 4) * 32
        for slot in range(2):
            cols = slice(128 * slot, 128 * slot + 128)
            outs = four_way(1, [(v_ref[p, 0, rows, cols], v_ref[p, 1, rows, cols]) for p in range(4)])
            for k, (re, im) in enumerate(outs):
                wr = twist[0, 256 * k + 32 * i : 256 * k + 32 * i + 32, :]
                wi = twist[1, 256 * k + 32 * i : 256 * k + 32 * i + 32, :]
                at = first_row + slot * 256 + inside
                out_ref[2 * k + half, at : at + 32, :] = (re * wr - im * wi).astype(BF)
                out_ref[2 * k + half, at + 128 : at + 160, :] = (re * wi + im * wr).astype(BF)


def own_kernel(spec, weight_ref, third_ref, twist, bank, out_ref, v_ref):
    norms = [jnp.zeros((8, 128), F32), jnp.zeros((8, 128), F32)]
    filter_segment(spec, weight_ref, third_ref, twist, bank, out_ref, 0, v_ref, norms)
    row = lax.broadcasted_iota(jnp.int32, (16, 128), 0)
    tail = jnp.zeros((16, 128), F32)
    for slot in range(2):
        left = jnp.broadcast_to(norms[slot].sum(axis=0, keepdims=True), (16, 128))
        for piece in range(3):
            rounded = left.astype(BF).astype(F32)
            tail = jnp.where(row == 3 * slot + piece, rounded, tail)
            left = left - rounded
    for dest in range(8):
        out_ref[dest, 512:528, :] = tail.astype(BF)


def other_kernel(spec, weight_ref, third_ref, twist, bank, half_ref, out_ref, v_ref):
    out_ref[:, :528, :] = half_ref[...]
    filter_segment(spec, weight_ref, third_ref, twist, bank, out_ref, 528, v_ref, None)


def last_kernel(in_ref, table_ref, out_ref):
    total = jnp.zeros((16, 128), F32)
    for s in range(8):
        total = total + in_ref[s, 512:528, :].astype(F32)
    row = lax.broadcasted_iota(jnp.int32, (16, 128), 0)
    scales = []
    for slot in range(2):
        mine = (row >= 3 * slot) & (row < 3 * slot + 3)
        sigma2 = jnp.sum(jnp.where(mine, total, 0.0), axis=(0, 1), keepdims=True)
        scales.append(1.0 / jnp.sqrt(NSAMP * sigma2))
    _, _, core = place()
    for pair in range(4):
        other, slot = pair // 2, pair % 2
        seg = (core + other) % 2
        at = 528 * other + 256 * slot
        parts = []
        for r in range(4):
            both = jnp.concatenate([in_ref[2 * r, at : at + 256, :], in_ref[2 * r + 1, at : at + 256, :]], axis=1)
            both = both.astype(F32)
            parts.append((both[:128], both[128:]))
        outs = four_way(1, parts)
        for p, (re, im) in enumerate(outs):
            right = jnp.concatenate([re, im], axis=0)
            hi = right.astype(BF)
            lo = (right - hi.astype(F32)).astype(BF)
            cos = dot_nt(table_ref[p, 0], hi) + dot_nt(table_ref[p, 0], lo)
            sin = dot_nt(table_ref[p, 1], hi) + dot_nt(table_ref[p, 1], lo)
            sr = cos[:, :128] - sin[:, 128:]
            si = sin[:, :128] + cos[:, 128:]
            out_ref[seg, slot, pl.ds(p, 256, stride=4), :] = jnp.sqrt(sr * sr + si * si) * scales[slot]


def call(kernel, ins, outs, specs, flops, moved, scratch=(), limit=16, space=VMEM):
    return pl.pallas_call(
        kernel,
        out_shape=outs,
        in_specs=specs,
        out_specs=space if isinstance(space, tuple) else jax.tree.map(lambda _: space, outs),
        scratch_shapes=list(scratch),
        compiler_params=pltpu.CompilerParams(vmem_limit_bytes=limit * MIB),
        cost_estimate=pl.CostEstimate(flops=flops, bytes_accessed=moved, transcendentals=0),
    )(*ins)


def shape(*dims, dtype=BF):
    return jax.ShapeDtypeStruct(dims, dtype)


def per_device(strain, gate_start, gate_span, asd, bank, assign):
    const = {name: jnp.asarray(value) for name, value in tables().items()}
    swap_core = [(i, i ^ 1) for i in range(16)]

    blk = (2, 2, 4, 16, 128)
    gated, *picked = call(
        gate_kernel, (strain, gate_start, gate_span, assign, bank), (shape(8, 128, 128), *[shape(2, *blk)] * 8),
        [ANY] * 5, 10**8, 4 * MIB,
        [
            pltpu.VMEM((128, 1024), F32), pltpu.VMEM((2, 32, 64, 128), F32), pltpu.SMEM((2, 1, 2), jnp.int32),
            pltpu.SMEM((2, 1, 2), jnp.int32), pltpu.SMEM((32,), jnp.int32), pltpu.SemaphoreType.DMA((5,)),
        ],
        limit=63,
    )
    columns = lax.all_to_all(gated, "seg", 0, 0)

    pieces = picked[:1]
    for (rz, rx), send in zip(OFFSETS[1:], picked[1:]):
        hop = [(i, (i // 4 + rx) % 4 * 4 + i % 4 ^ 2 * rz) for i in range(16)]
        pieces.append(lax.ppermute(send, "tmpl", hop))
    cross, packed = call(
        pack_kernel, pieces, (shape(8, *blk), shape(8, 128, dtype=F32)), [ANY] * 8, 1, 10 * MIB,
        [pltpu.SemaphoreType.DMA((8,))], limit=63, space=(ANY, VMEM),
    )
    crossed = lax.ppermute(cross, "tmpl", swap_core)
    ordered, weight, twist, token = call(
        assemble_kernel, (*pieces, crossed, asd, const["back"], const["shift"]),
        (
            shape(16, *blk), shape(4, 256, 128, dtype=F32), shape(2, 1024, 128, dtype=F32), shape(8, 128, dtype=F32),
        ),
        [ANY] * 12, 1, 10 * MIB,
        [
            pltpu.VMEM((4, 256, 128), F32), pltpu.VMEM((2, 1024, 128), F32), pltpu.VMEM((1024, 128), F32),
            pltpu.VMEM((2, 1024, 128), F32), pltpu.VMEM((2, 1024, 128), F32), pltpu.SemaphoreType.DMA((21,)),
        ],
        limit=63, space=(ANY, ANY, ANY, VMEM),
    )
    turned = call(
        first_kernel, (columns, const["first"], const["turn"], packed), shape(8, 2, 4, 32, 128), [VMEM] + [ANY] * 3,
        3 * 10**8, 4 * MIB,
        [
            pltpu.VMEM((4, 2, 2, 256, 256), BF), pltpu.VMEM((2, 48, 1024), F32),
            pltpu.VMEM((4, 2, 128, 256), F32), pltpu.SemaphoreType.DMA((5,)),
        ],
        limit=63,
    )
    own = lax.all_to_all(turned, "seg", 0, 0)
    spec = call(
        second_kernel, (own, const["second"], token), shape(2, 1024, 128, dtype=F32),
        [VMEM] * 2 + [ANY], 1, 1, [pltpu.VMEM((4, 256, 256), F32)],
    )
    other_spec = lax.ppermute(spec, "tmpl", swap_core)
    half = call(
        own_kernel,
        (spec, weight, const["third"], twist, ordered),
        shape(8, 528, 128), [VMEM] * 5, 2 * 10**9, 10 * MIB, [pltpu.VMEM((4, 2, 256, 256), F32)],
    )
    inner = call(
        other_kernel,
        (other_spec, weight, const["third"], twist, ordered, half),
        shape(8, 1040, 128), [VMEM] * 6, 2 * 10**9, 10 * MIB, [pltpu.VMEM((4, 2, 256, 256), F32)],
    )
    series = lax.all_to_all(inner, "seg", 0, 0)
    return call(
        last_kernel, (series, const["last"]), shape(2, 2, 1024, 128, dtype=F32), [VMEM] * 2, 3 * 10**9, 6 * MIB
    )


def solution(mesh):
    placed = (
        P(None, "seg", None),
        P(None, "seg", None),
        P(None, "seg", None),
        P(None, "seg"),
        P(None, None, "tmpl", "seg"),
        P(),
    )
    return jax.shard_map(
        per_device,
        mesh=mesh,
        in_specs=placed,
        out_specs=P(None, "tmpl", None, "seg"),
        check_vma=False,
    )
```

```python
import functools
import math

import jax
import jax.numpy as jnp
import numpy as np
from jax import lax
from jax.experimental import pallas as pl
from jax.experimental.pallas import tpu as pltpu
from jax.sharding import PartitionSpec as P

BF = jnp.bfloat16
F32 = jnp.float32
NSAMP = 1048576
VMEM = pl.BlockSpec(memory_space=pltpu.VMEM)
SMEM = pl.BlockSpec(memory_space=pltpu.SMEM)
ANY = pl.BlockSpec(memory_space=pl.ANY)
MIB = 1 << 20
OFFSETS = [(0, 0), (1, 0), (1, 2), (1, 1), (1, 3), (0, 2), (0, 1), (0, 3)]


def phases(product, count):
    angle = 2.0 * math.pi / count * (product % count).astype(np.float64)
    return np.cos(angle), np.sin(angle)


def split_hi_lo(table):
    table = table.astype(np.float32)
    hi = table.astype(jnp.bfloat16)
    lo = (table - hi.astype(np.float32)).astype(jnp.bfloat16)
    return hi, lo


@functools.cache
def tables():
    q = np.arange(256)
    c, s = phases(q[:, None] * q[None, :], 256)
    first = np.stack(split_hi_lo(np.concatenate([c, -s], axis=1)))
    k2 = np.arange(1024)
    rows = np.concatenate([4 * np.arange(32), 128 * np.arange(8), np.arange(8), 1024 * np.arange(8)])
    c, s = phases(rows[:, None] * k2[None, :], NSAMP)
    turn = np.stack([c, -s]).astype(np.float32)
    c, s = phases(q[:, None] * q[None, :], 256)
    (ch, cl), (sh, sl) = split_hi_lo(c), split_hi_lo(s)
    second = np.concatenate([ch, sh, cl, sl], axis=1)
    c, s = phases(q[:, None] * np.arange(4)[None, :], 1024)
    lag = np.zeros((256, 128), np.float32)
    lag[:, 0:8:2], lag[:, 1:8:2] = c, -s
    third = []
    for p in range(4):
        c, s = phases(q[:, None] * (4 * q[None, :] + p), 1024)
        c, s = c.astype(np.float32), s.astype(np.float32)
        third.append(np.stack([np.concatenate([c, -s], 1), np.concatenate([s, c], 1)]))
    n1 = np.arange(1024)
    c, s = phases(n1[:, None] * np.arange(128)[None, :], NSAMP)
    back = np.stack([c, s]).astype(np.float32)
    c, s = phases(n1[:, None] * 128 * np.arange(128)[None, :], NSAMP)
    shift = np.stack([c, s]).astype(np.float32)
    last = []
    for p in range(4):
        c, s = phases((4 * q[:, None] + p) * q[None, :], 1024)
        last.append(np.stack([c, s]).astype(np.float32))
    return dict(
        first=first,
        turn=turn,
        second=second,
        lag=lag,
        third=np.stack(third).astype(jnp.bfloat16),
        back=back,
        shift=shift,
        last=np.stack(last).astype(jnp.bfloat16),
    )


def dot(a, b):
    return jnp.dot(a, b, preferred_element_type=F32)


def dot_nt(a, b):
    return lax.dot_general(a, b, (((1,), (1,)), ((), ())), preferred_element_type=F32)


def place():
    t = lax.axis_index("tmpl")
    return t // 4, (t // 2) % 2, t % 2


def gate_kernel(
    strain_ref, start_any, span_any, assign_any, bank_any, out_ref, *rest
):
    pick_refs, rest = rest[:8], rest[8:]
    strain, bank_ref, start_ref, span_ref, assign_ref, sems = rest
    x, z, core = place()
    copies = [
        pltpu.make_async_copy(start_any, start_ref, sems.at[0]),
        pltpu.make_async_copy(span_any, span_ref, sems.at[1]),
        pltpu.make_async_copy(strain_ref.at[core], strain, sems.at[2]),
        pltpu.make_async_copy(assign_any, assign_ref, sems.at[3]),
        pltpu.make_async_copy(bank_any, bank_ref, sems.at[4]),
    ]
    for copy in copies:
        copy.start()
    row = lax.broadcasted_iota(jnp.int32, (128, 128), 0)
    lane = lax.broadcasted_iota(jnp.int32, (128, 128), 1)
    order = jnp.where(lane == row % 32 * 4 + row // 32, 1.0, 0.0).astype(BF)
    pick = jnp.where(row == lane % 32 * 4 + lane // 32, 1.0, 0.0).astype(BF)
    for copy in copies[:3]:
        copy.wait()
    blocks = []
    for dest in range(8):
        value = strain[:, 128 * dest : 128 * dest + 128]
        sample = row * 1024 + (lane + 128 * dest)
        for g in range(2):
            first = start_ref[core, 0, g]
            inside = (sample >= first) & (sample < first + span_ref[core, 0, g])
            value = jnp.where(inside, 0.0, value)
        blocks.append(value.astype(BF))
    picked = dot(jnp.concatenate(blocks, axis=0), pick).astype(BF)
    wide = jnp.concatenate([picked[128 * dest : 128 * dest + 128] for dest in range(8)], axis=1)
    ordered = dot(order, wide).astype(BF)
    for dest in range(8):
        out_ref[dest] = ordered[:, 128 * dest : 128 * dest + 128]

    for copy in copies[3:5]:
        copy.wait()
    for i in range(16):
        (rz, rx), rc = OFFSETS[i // 2], i % 2
        dest = ((x + rx) % 4) * 4 + (z + rz) % 2 * 2 + (core + rc) % 2
        for slot in range(2):
            chosen = assign_ref[2 * dest + slot]
            for part in range(2):
                for p in range(4):
                    value = bank_ref[part, chosen, pl.ds(p, 16, stride=4), :].astype(BF)
                    pick_refs[i // 2][rc, slot, part, p] = value


def prepare_kernel(asd_any, back_any, shift_any, weight_ref, twist_ref, asd_ref, back_ref, shift_ref, sems):
    copies = [
        pltpu.make_async_copy(asd_any, asd_ref, sems.at[0]),
        pltpu.make_async_copy(back_any, back_ref, sems.at[1]),
        pltpu.make_async_copy(shift_any, shift_ref, sems.at[2]),
    ]
    for copy in copies:
        copy.start()
    copies[0].wait()
    for p in range(4):
        asd = asd_ref[pl.ds(p, 256, stride=4), :]
        weight_ref[p] = 1.0 / (asd * asd)
    copies[1].wait()
    copies[2].wait()
    own = lax.broadcasted_iota(jnp.int32, (128, 128), 1) == lax.axis_index("seg")
    for i in range(8):
        rows = slice(128 * i, 128 * i + 128)
        shift = [jnp.sum(jnp.where(own, shift_ref[part, rows, :], 0.0), axis=1, keepdims=True) for part in range(2)]
        re, im = back_ref[0, rows, :], back_ref[1, rows, :]
        twist_ref[0, rows, :] = re * shift[0] - im * shift[1]
        twist_ref[1, rows, :] = re * shift[1] + im * shift[0]


def pack_kernel(*refs):
    piece_refs, out_ref, token_ref, sems = refs[:8], *refs[8:]
    token_ref[...] = jnp.zeros_like(token_ref)
    copies = [pltpu.make_async_copy(piece_refs[i].at[1], out_ref.at[i], sems.at[i]) for i in range(8)]
    for copy in copies:
        copy.start()
    for copy in copies:
        copy.wait()


def four_way(sign, parts):
    (ar, ai), (br, bi), (cr, ci), (dr, di) = parts
    sr, si = ar + cr, ai + ci
    tr, ti = ar - cr, ai - ci
    ur, ui = br + dr, bi + di
    vr, vi = br - dr, bi - di
    if sign > 0:
        wr, wi = -vi, vr
    else:
        wr, wi = vi, -vr
    return ((sr + ur, si + ui), (tr + wr, ti + wi), (sr - ur, si - ui), (tr - wr, ti - wi))


def first_kernel(cols_ref, table_ref, turn_ref, after_ref, out_ref, z_ref):
    del after_ref
    turned = jnp.concatenate([cols_ref[:, 32 * r : 32 * r + 32, :].reshape(256, 128).T for r in range(4)], axis=0)
    z_ref[...] = dot(turned, table_ref[0]) + dot(turned, table_ref[1])
    seg = 32 + lax.axis_index("seg")
    seg_re, seg_im = turn_ref[0, pl.ds(seg, 1), :], turn_ref[1, pl.ds(seg, 1), :]
    for r1 in range(4):
        low_re, low_im = turn_ref[0, 40 + r1 : 41 + r1, :], turn_ref[1, 40 + r1 : 41 + r1, :]
        base_re = low_re * seg_re - low_im * seg_im
        base_im = low_re * seg_im + low_im * seg_re
        for i in range(2):
            at = slice(16 * i, 16 * i + 16)
            rows = slice(32 * r1 + 16 * i, 32 * r1 + 16 * i + 16)
            fr, fi = turn_ref[0, at, :], turn_ref[1, at, :]
            tr = fr * base_re - fi * base_im
            ti = fr * base_im + fi * base_re
            sums = []
            for r in range(4):
                here = slice(128 * r + rows.start, 128 * r + rows.stop)
                re, im = z_ref[here, :256], z_ref[here, 256:]
                if r > 0:
                    pr, pi = turn_ref[0, 48 + r : 49 + r, :256], turn_ref[1, 48 + r : 49 + r, :256]
                    re, im = re * pr - im * pi, re * pi + im * pr
                sums.append((re, im))
            outs = four_way(-1, sums)
            for k, (re, im) in enumerate(outs):
                wr, wi = tr[:, 256 * k : 256 * k + 256], ti[:, 256 * k : 256 * k + 256]
                done = ((re * wr - im * wi).astype(BF), (re * wi + im * wr).astype(BF))
                for half in range(2):
                    for part in range(2):
                        out_ref[2 * k + half, part, r1, at] = done[part][:, 128 * half : 128 * half + 128]


def second_kernel(own_ref, table_ref, lag_ref, after_ref, spec_ref, z_ref):
    del after_ref
    for r in range(4):
        re = own_ref[:, 0, r].reshape(256, 128)
        im = own_ref[:, 1, r].reshape(256, 128)
        right = jnp.concatenate([jnp.concatenate([re, im], axis=1), jnp.concatenate([im, -re], axis=1)], axis=0)
        z_ref[r] = dot(table_ref[:, :512], right) + dot(table_ref[:, 512:], right)
    for i in range(8):
        rows = slice(32 * i, 32 * i + 32)
        sums = [(z_ref[0, rows, :128], z_ref[0, rows, 128:])]
        for r in range(1, 4):
            pr, pi = lag_ref[rows, 2 * r : 2 * r + 1], lag_ref[rows, 2 * r + 1 : 2 * r + 2]
            re, im = z_ref[r, rows, :128], z_ref[r, rows, 128:]
            sums.append((re * pr - im * pi, re * pi + im * pr))
        for k, parts in enumerate(four_way(-1, sums)):
            for part in range(2):
                spec_ref[part, 256 * k + 32 * i : 256 * k + 32 * i + 32, :] = parts[part]


def assemble_kernel(*refs):
    piece_refs, cross_ref, _, bank, sems = refs[:8], *refs[8:]
    x, z, core = place()
    copies = []
    for i, (rz, rx) in enumerate(OFFSETS):
        for rc in range(2):
            src = piece_refs[i].at[0] if rc == 0 else cross_ref.at[i]
            origin = ((x + 4 - rx) % 4) * 4 + (z + rz) % 2 * 2 + (core + rc) % 2
            copies.append(pltpu.make_async_copy(src, bank.at[origin], sems.at[len(copies)]))
    for copy in copies:
        copy.start()
    for copy in copies:
        copy.wait()


def filter_segment(spec, weight_ref, third_ref, twist, bank, out_ref, first_row, v_ref, norms):
    for p in range(4):
        weight = weight_ref[p]
        sr = spec[0, pl.ds(p, 256, stride=4), :] * weight
        si = spec[1, pl.ds(p, 256, stride=4), :] * weight
        lanes_re, lanes_im = [], []
        for slot in range(2):
            hr = bank[:, slot, 0, p].reshape(256, 128).astype(F32)
            hi = bank[:, slot, 1, p].reshape(256, 128).astype(F32)
            if norms is not None:
                power = (hr * hr + hi * hi) * weight
                norms[slot] = norms[slot] + power.reshape(32, 8, 128).sum(axis=0)
            lanes_re.append((sr * hr + si * hi).astype(BF))
            lanes_im.append((si * hr - sr * hi).astype(BF))
        right = jnp.concatenate([jnp.concatenate(lanes_re, axis=1), jnp.concatenate(lanes_im, axis=1)], axis=0)
        v_ref[p, 0] = dot(third_ref[p, 0], right)
        v_ref[p, 1] = dot(third_ref[p, 1], right)
    for i in range(8):
        rows = slice(32 * i, 32 * i + 32)
        half, inside = i // 4, (i % 4) * 32
        for slot in range(2):
            cols = slice(128 * slot, 128 * slot + 128)
            outs = four_way(1, [(v_ref[p, 0, rows, cols], v_ref[p, 1, rows, cols]) for p in range(4)])
            for k, (re, im) in enumerate(outs):
                wr = twist[0, 256 * k + 32 * i : 256 * k + 32 * i + 32, :]
                wi = twist[1, 256 * k + 32 * i : 256 * k + 32 * i + 32, :]
                at = first_row + slot * 256 + inside
                out_ref[2 * k + half, at : at + 32, :] = (re * wr - im * wi).astype(BF)
                out_ref[2 * k + half, at + 128 : at + 160, :] = (re * wi + im * wr).astype(BF)


def own_kernel(spec, weight_ref, third_ref, twist, bank, out_ref, v_ref):
    norms = [jnp.zeros((8, 128), F32), jnp.zeros((8, 128), F32)]
    filter_segment(spec, weight_ref, third_ref, twist, bank, out_ref, 0, v_ref, norms)
    row = lax.broadcasted_iota(jnp.int32, (16, 128), 0)
    tail = jnp.zeros((16, 128), F32)
    for slot in range(2):
        left = jnp.broadcast_to(norms[slot].sum(axis=0, keepdims=True), (16, 128))
        for piece in range(3):
            rounded = left.astype(BF).astype(F32)
            tail = jnp.where(row == 3 * slot + piece, rounded, tail)
            left = left - rounded
    for dest in range(8):
        out_ref[dest, 512:528, :] = tail.astype(BF)


def other_kernel(spec, weight_ref, third_ref, twist, bank, half_ref, out_ref, v_ref):
    out_ref[:, :528, :] = half_ref[...]
    filter_segment(spec, weight_ref, third_ref, twist, bank, out_ref, 528, v_ref, None)


def last_kernel(in_ref, table_ref, out_any, out_ref, sems):
    total = jnp.zeros((16, 128), F32)
    for s in range(8):
        total = total + in_ref[s, 512:528, :].astype(F32)
    row = lax.broadcasted_iota(jnp.int32, (16, 128), 0)
    scales = []
    for slot in range(2):
        mine = (row >= 3 * slot) & (row < 3 * slot + 3)
        sigma2 = jnp.sum(jnp.where(mine, total, 0.0), axis=(0, 1), keepdims=True)
        scales.append(1.0 / jnp.sqrt(NSAMP * sigma2))
    _, _, core = place()
    copies = []
    for pair in range(4):
        other, slot = pair // 2, pair % 2
        seg = (core + other) % 2
        at = 528 * other + 256 * slot
        parts = []
        for r in range(4):
            both = jnp.concatenate([in_ref[2 * r, at : at + 256, :], in_ref[2 * r + 1, at : at + 256, :]], axis=1)
            both = both.astype(F32)
            parts.append((both[:128], both[128:]))
        outs = four_way(1, parts)
        for p, (re, im) in enumerate(outs):
            right = jnp.concatenate([re, im], axis=0)
            hi = right.astype(BF)
            lo = (right - hi.astype(F32)).astype(BF)
            cos = dot_nt(table_ref[p, 0], hi) + dot_nt(table_ref[p, 0], lo)
            sin = dot_nt(table_ref[p, 1], hi) + dot_nt(table_ref[p, 1], lo)
            sr = cos[:, :128] - sin[:, 128:]
            si = sin[:, :128] + cos[:, 128:]
            out_ref[pair, pl.ds(p, 256, stride=4), :] = jnp.sqrt(sr * sr + si * si) * scales[slot]
        copies.append(pltpu.make_async_copy(out_ref.at[pair], out_any.at[seg, slot], sems.at[pair]))
        copies[pair].start()
    for copy in copies:
        copy.wait()


def call(kernel, ins, outs, specs, flops, moved, scratch=(), limit=16, space=VMEM):
    return pl.pallas_call(
        kernel,
        out_shape=outs,
        in_specs=specs,
        out_specs=space if isinstance(space, tuple) else jax.tree.map(lambda _: space, outs),
        scratch_shapes=list(scratch),
        compiler_params=pltpu.CompilerParams(vmem_limit_bytes=limit * MIB),
        cost_estimate=pl.CostEstimate(flops=flops, bytes_accessed=moved, transcendentals=0),
    )(*ins)


def shape(*dims, dtype=BF):
    return jax.ShapeDtypeStruct(dims, dtype)


def per_device(strain, gate_start, gate_span, asd, bank, assign):
    const = {name: jnp.asarray(value) for name, value in tables().items()}
    swap_core = [(i, i ^ 1) for i in range(16)]

    blk = (2, 2, 4, 16, 128)
    gated, *picked = call(
        gate_kernel, (strain, gate_start, gate_span, assign, bank), (shape(8, 128, 128), *[shape(2, *blk)] * 8),
        [ANY] * 5, 10**8, 4 * MIB,
        [
            pltpu.VMEM((128, 1024), F32), pltpu.VMEM((2, 32, 64, 128), F32), pltpu.SMEM((2, 1, 2), jnp.int32),
            pltpu.SMEM((2, 1, 2), jnp.int32), pltpu.SMEM((32,), jnp.int32), pltpu.SemaphoreType.DMA((5,)),
        ],
        limit=63,
    )
    columns = lax.all_to_all(gated, "seg", 0, 0)

    pieces = picked[:1]
    for (rz, rx), send in zip(OFFSETS[1:], picked[1:]):
        hop = [(i, (i // 4 + rx) % 4 * 4 + i % 4 ^ 2 * rz) for i in range(16)]
        pieces.append(lax.ppermute(send, "tmpl", hop))
    cross, token = call(
        pack_kernel, pieces, (shape(8, *blk), shape(8, 128, dtype=F32)), [ANY] * 8, 1, 10 * MIB,
        [pltpu.SemaphoreType.DMA((8,))], limit=8, space=(ANY, VMEM),
    )
    crossed = lax.ppermute(cross, "tmpl", swap_core)
    weight, twist = call(
        prepare_kernel, (asd, const["back"], const["shift"]),
        (shape(4, 256, 128, dtype=F32), shape(2, 1024, 128, dtype=F32)), [ANY] * 3, 1, 10 * MIB,
        [
            pltpu.VMEM((1024, 128), F32), pltpu.VMEM((2, 1024, 128), F32), pltpu.VMEM((2, 1024, 128), F32),
            pltpu.SemaphoreType.DMA((3,)),
        ],
        limit=63,
    )
    ordered = call(
        assemble_kernel, (*pieces, crossed, weight), shape(16, *blk), [ANY] * 10, 1, 10 * MIB,
        [pltpu.SemaphoreType.DMA((16,))], limit=8,
    )
    turned = call(
        first_kernel, (columns, const["first"], const["turn"], token),
        shape(8, 2, 4, 32, 128), [VMEM] * 3 + [ANY], 3 * 10**8, 4 * MIB, [pltpu.VMEM((512, 512), F32)],
    )
    own = lax.all_to_all(turned, "seg", 0, 0)
    spec = call(
        second_kernel, (own, const["second"], const["lag"], ordered), shape(2, 1024, 128, dtype=F32),
        [VMEM] * 3 + [ANY], 1, 1, [pltpu.VMEM((4, 256, 256), F32)],
    )
    other_spec = lax.ppermute(spec, "tmpl", swap_core)
    half = call(
        own_kernel,
        (spec, weight, const["third"], twist, ordered),
        shape(8, 528, 128), [VMEM] * 5, 2 * 10**9, 10 * MIB, [pltpu.VMEM((4, 2, 256, 256), F32)],
    )
    inner = call(
        other_kernel,
        (other_spec, weight, const["third"], twist, ordered, half),
        shape(8, 1040, 128), [VMEM] * 6, 2 * 10**9, 10 * MIB, [pltpu.VMEM((4, 2, 256, 256), F32)],
    )
    series = lax.all_to_all(inner, "seg", 0, 0)
    return call(
        last_kernel, (series, const["last"]), shape(2, 2, 1024, 128, dtype=F32), [VMEM] * 2, 3 * 10**9, 6 * MIB,
        [pltpu.VMEM((4, 1024, 128), F32), pltpu.SemaphoreType.DMA((4,))], space=ANY,
    )


def solution(mesh):
    placed = (
        P(None, "seg", None),
        P(None, "seg", None),
        P(None, "seg", None),
        P(None, "seg"),
        P(None, None, "tmpl", "seg"),
        P(),
    )
    return jax.shard_map(
        per_device,
        mesh=mesh,
        in_specs=placed,
        out_specs=P(None, "tmpl", None, "seg"),
        check_vma=False,
    )
```

```python
import functools
import math

import jax
import jax.numpy as jnp
import numpy as np
from jax import lax
from jax.experimental import pallas as pl
from jax.experimental.pallas import tpu as pltpu
from jax.sharding import PartitionSpec as P

BF = jnp.bfloat16
F32 = jnp.float32
NSAMP = 1048576
VMEM = pl.BlockSpec(memory_space=pltpu.VMEM)
SMEM = pl.BlockSpec(memory_space=pltpu.SMEM)
ANY = pl.BlockSpec(memory_space=pl.ANY)
MIB = 1 << 20
OFFSETS = [(0, 0), (1, 0), (1, 2), (0, 2), (0, 1), (1, 1), (1, 3), (0, 3)]


def phases(product, count):
    angle = 2.0 * math.pi / count * (product % count).astype(np.float64)
    return np.cos(angle), np.sin(angle)


def split_hi_lo(table):
    table = table.astype(np.float32)
    hi = table.astype(jnp.bfloat16)
    lo = (table - hi.astype(np.float32)).astype(jnp.bfloat16)
    return hi, lo


@functools.cache
def tables():
    q = np.arange(256)
    c, s = phases(q[:, None] * q[None, :], 256)
    hi, lo = split_hi_lo(np.concatenate([c, -s], axis=1))
    first = np.concatenate([hi, lo], axis=1).astype(np.float32)
    k2 = np.arange(1024)
    rows = np.concatenate([4 * np.arange(32), 128 * np.arange(8), np.arange(8), 1024 * np.arange(8)])
    c, s = phases(rows[:, None] * k2[None, :], NSAMP)
    turn = np.concatenate([c, -s]).astype(np.float32)
    first = np.concatenate([first, turn], axis=0)
    c, s = phases(q[:, None] * q[None, :], 256)
    (ch, cl), (sh, sl) = split_hi_lo(c), split_hi_lo(s)
    second = np.concatenate([ch, sh, cl, sl], axis=1)
    c, s = phases(q[:, None] * np.arange(4)[None, :], 1024)
    lag = np.zeros((256, 128), np.float32)
    lag[:, 0:8:2], lag[:, 1:8:2] = c, -s
    second = np.concatenate([second.astype(np.float32), lag], axis=1)
    third = []
    for p in range(4):
        c, s = phases(q[:, None] * (4 * q[None, :] + p), 1024)
        c, s = c.astype(np.float32), s.astype(np.float32)
        third.append(np.concatenate([c, s], 1))
    n1 = np.arange(1024)
    c, s = phases(n1[:, None] * np.arange(128)[None, :], NSAMP)
    back = np.stack([c, s]).astype(np.float32)
    c, s = phases(n1[:, None] * 128 * np.arange(128)[None, :], NSAMP)
    shift = np.stack([c, s]).astype(np.float32)
    last = []
    for p in range(4):
        c, s = phases((4 * q[:, None] + p) * q[None, :], 1024)
        last.append(np.stack([c, s]).astype(np.float32))
    return dict(
        first=first,
        second=second,
        third=np.stack(third).astype(jnp.bfloat16),
        back=back,
        shift=shift,
        last=np.stack(last).astype(jnp.bfloat16),
    )


def dot(a, b):
    return jnp.dot(a, b, preferred_element_type=F32)


def dot_nt(a, b):
    return lax.dot_general(a, b, (((1,), (1,)), ((), ())), preferred_element_type=F32)


def place():
    t = lax.axis_index("tmpl")
    return t // 4, (t // 2) % 2, t % 2


def gate_kernel(
    strain_ref, start_any, span_any, assign_any, bank_any, asd_any, back_any, shift_any,
    out_ref, weight_ref, twist_ref, *rest
):
    pick_refs, rest = rest[:8], rest[8:]
    strain, bank_ref, start_ref, span_ref, assign_ref, asd_ref, back_ref, shift_ref, sems = rest
    x, z, core = place()
    copies = [
        pltpu.make_async_copy(start_any, start_ref, sems.at[0]),
        pltpu.make_async_copy(span_any, span_ref, sems.at[1]),
        pltpu.make_async_copy(strain_ref.at[core], strain, sems.at[2]),
        pltpu.make_async_copy(assign_any, assign_ref, sems.at[3]),
        pltpu.make_async_copy(bank_any, bank_ref, sems.at[4]),
        pltpu.make_async_copy(asd_any, asd_ref, sems.at[5]),
        pltpu.make_async_copy(back_any, back_ref, sems.at[6]),
        pltpu.make_async_copy(shift_any, shift_ref, sems.at[7]),
    ]
    for copy in copies:
        copy.start()
    row = lax.broadcasted_iota(jnp.int32, (128, 128), 0)
    lane = lax.broadcasted_iota(jnp.int32, (128, 128), 1)
    order = jnp.where(lane == row % 32 * 4 + row // 32, 1.0, 0.0).astype(BF)
    pick = jnp.where(row == lane % 32 * 4 + lane // 32, 1.0, 0.0).astype(BF)
    for copy in copies[:3]:
        copy.wait()
    blocks = []
    for dest in range(8):
        value = strain[:, 128 * dest : 128 * dest + 128]
        sample = row * 1024 + (lane + 128 * dest)
        for g in range(2):
            first = start_ref[core, 0, g]
            inside = (sample >= first) & (sample < first + span_ref[core, 0, g])
            value = jnp.where(inside, 0.0, value)
        blocks.append(value.astype(BF))
    picked = dot(jnp.concatenate(blocks, axis=0), pick).astype(BF)
    wide = jnp.concatenate([picked[128 * dest : 128 * dest + 128] for dest in range(8)], axis=1)
    ordered = dot(order, wide).astype(BF)
    for dest in range(8):
        out_ref[dest] = ordered[:, 128 * dest : 128 * dest + 128]

    for copy in copies[3:5]:
        copy.wait()
    for i in range(16):
        (rz, rx), rc = OFFSETS[i // 2], i % 2
        dest = ((x + rx) % 4) * 4 + (z + rz) % 2 * 2 + (core + rc) % 2
        for slot in range(2):
            chosen = assign_ref[2 * dest + slot]
            for part in range(2):
                for p in range(4):
                    value = bank_ref[part, chosen, pl.ds(p, 16, stride=4), :].astype(BF)
                    pick_refs[i // 2][rc, slot, part, p] = value

    for copy in copies[5:]:
        copy.wait()
    for p in range(4):
        asd = asd_ref[pl.ds(p, 256, stride=4), :]
        weight_ref[p] = 1.0 / (asd * asd)
    own = lane == lax.axis_index("seg")
    for i in range(8):
        rows = slice(128 * i, 128 * i + 128)
        shift = [jnp.sum(jnp.where(own, shift_ref[part, rows, :], 0.0), axis=1, keepdims=True) for part in range(2)]
        re, im = back_ref[0, rows, :], back_ref[1, rows, :]
        twist_ref[0, rows, :] = re * shift[0] - im * shift[1]
        twist_ref[1, rows, :] = re * shift[1] + im * shift[0]


def pack_kernel(*refs):
    piece_refs, out_refs, sems = refs[:8], refs[9:13], refs[13]
    copies = [pltpu.make_async_copy(piece_refs[i].at[1], out_refs[i // 2].at[i % 2], sems.at[i]) for i in range(8)]
    for copy in copies:
        copy.start()
    for copy in copies:
        copy.wait()


def four_way(sign, parts):
    (ar, ai), (br, bi), (cr, ci), (dr, di) = parts
    sr, si = ar + cr, ai + ci
    tr, ti = ar - cr, ai - ci
    ur, ui = br + dr, bi + di
    vr, vi = br - dr, bi - di
    if sign > 0:
        wr, wi = -vi, vr
    else:
        wr, wi = vi, -vr
    return ((sr + ur, si + ui), (tr + wr, ti + wi), (sr - ur, si - ui), (tr - wr, ti - wi))


def first_kernel(cols_ref, table_ref, *refs):
    out_ref, token_ref, z_ref = refs[-3:]
    token_ref[...] = jnp.zeros_like(token_ref)
    turn_ref = table_ref.at[256:368].reshape(2, 56, 1024)
    turned = jnp.concatenate([cols_ref[:, 32 * r : 32 * r + 32, :].reshape(256, 128).T for r in range(4)], axis=0)
    z_ref[...] = dot(turned, table_ref[:256, :512].astype(BF)) + dot(turned, table_ref[:256, 512:].astype(BF))
    seg = 32 + lax.axis_index("seg")
    seg_re, seg_im = turn_ref[0, pl.ds(seg, 1), :], turn_ref[1, pl.ds(seg, 1), :]
    for r1 in range(4):
        low_re, low_im = turn_ref[0, 40 + r1 : 41 + r1, :], turn_ref[1, 40 + r1 : 41 + r1, :]
        base_re = low_re * seg_re - low_im * seg_im
        base_im = low_re * seg_im + low_im * seg_re
        for i in range(2):
            at = slice(16 * i, 16 * i + 16)
            rows = slice(32 * r1 + 16 * i, 32 * r1 + 16 * i + 16)
            fr, fi = turn_ref[0, at, :], turn_ref[1, at, :]
            tr = fr * base_re - fi * base_im
            ti = fr * base_im + fi * base_re
            sums = []
            for r in range(4):
                here = slice(128 * r + rows.start, 128 * r + rows.stop)
                re, im = z_ref[here, :256], z_ref[here, 256:]
                if r > 0:
                    pr, pi = turn_ref[0, 48 + r : 49 + r, :256], turn_ref[1, 48 + r : 49 + r, :256]
                    re, im = re * pr - im * pi, re * pi + im * pr
                sums.append((re, im))
            outs = four_way(-1, sums)
            for k, (re, im) in enumerate(outs):
                wr, wi = tr[:, 256 * k : 256 * k + 256], ti[:, 256 * k : 256 * k + 256]
                done = ((re * wr - im * wi).astype(BF), (re * wi + im * wr).astype(BF))
                for half in range(2):
                    for part in range(2):
                        out_ref[2 * k + half, part, r1, at] = done[part][:, 128 * half : 128 * half + 128]


def second_kernel(own_ref, table_ref, after_ref, spec_ref, z_ref):
    del after_ref
    hi, lo = table_ref[:, :512].astype(BF), table_ref[:, 512:1024].astype(BF)
    for r in range(4):
        re = own_ref[:, 0, r].reshape(256, 128)
        im = own_ref[:, 1, r].reshape(256, 128)
        right = jnp.concatenate([jnp.concatenate([re, im], axis=1), jnp.concatenate([im, -re], axis=1)], axis=0)
        z_ref[r] = dot(hi, right) + dot(lo, right)
    for i in range(8):
        rows = slice(32 * i, 32 * i + 32)
        sums = [(z_ref[0, rows, :128], z_ref[0, rows, 128:])]
        for r in range(1, 4):
            at = 1024 + 2 * r
            pr, pi = table_ref[rows, at : at + 1], table_ref[rows, at + 1 : at + 2]
            re, im = z_ref[r, rows, :128], z_ref[r, rows, 128:]
            sums.append((re * pr - im * pi, re * pi + im * pr))
        for k, parts in enumerate(four_way(-1, sums)):
            for part in range(2):
                spec_ref[part, 256 * k + 32 * i : 256 * k + 32 * i + 32, :] = parts[part]


def assemble_kernel(*refs):
    piece_refs, cross_refs, bank, sems = refs[:8], refs[8:12], *refs[12:]
    x, z, core = place()
    copies = []
    for i, (rz, rx) in enumerate(OFFSETS):
        for rc in range(2):
            src = piece_refs[i].at[0] if rc == 0 else cross_refs[i // 2].at[i % 2]
            origin = ((x + 4 - rx) % 4) * 4 + (z + rz) % 2 * 2 + (core + rc) % 2
            copies.append(pltpu.make_async_copy(src, bank.at[origin], sems.at[len(copies)]))
    for copy in copies:
        copy.start()
    for copy in copies:
        copy.wait()


def filter_segment(spec, weight_ref, third_ref, twist, bank, out_ref, first_row, v_ref, norms):
    for p in range(4):
        weight = weight_ref[p]
        sr = spec[0, pl.ds(p, 256, stride=4), :] * weight
        si = spec[1, pl.ds(p, 256, stride=4), :] * weight
        lanes_re, lanes_im = [], []
        for slot in range(2):
            hr = bank[:, slot, 0, p].reshape(256, 128).astype(F32)
            hi = bank[:, slot, 1, p].reshape(256, 128).astype(F32)
            if norms is not None:
                power = (hr * hr + hi * hi) * weight
                norms[slot] = norms[slot] + power.reshape(32, 8, 128).sum(axis=0)
            lanes_re.append((sr * hr + si * hi).astype(BF))
            lanes_im.append((si * hr - sr * hi).astype(BF))
        re, im = jnp.concatenate(lanes_re, axis=1), jnp.concatenate(lanes_im, axis=1)
        v_ref[p, 0] = dot(third_ref[p], jnp.concatenate([re, -im], axis=0))
        v_ref[p, 1] = dot(third_ref[p], jnp.concatenate([im, re], axis=0))
    for i in range(8):
        rows = slice(32 * i, 32 * i + 32)
        half, inside = i // 4, (i % 4) * 32
        for slot in range(2):
            cols = slice(128 * slot, 128 * slot + 128)
            outs = four_way(1, [(v_ref[p, 0, rows, cols], v_ref[p, 1, rows, cols]) for p in range(4)])
            for k, (re, im) in enumerate(outs):
                wr = twist[0, 256 * k + 32 * i : 256 * k + 32 * i + 32, :]
                wi = twist[1, 256 * k + 32 * i : 256 * k + 32 * i + 32, :]
                at = first_row + slot * 256 + inside
                out_ref[2 * k + half, at : at + 32, :] = (re * wr - im * wi).astype(BF)
                out_ref[2 * k + half, at + 128 : at + 160, :] = (re * wi + im * wr).astype(BF)


def own_kernel(spec, weight_ref, third_ref, twist, bank, out_ref, v_ref):
    norms = [jnp.zeros((8, 128), F32), jnp.zeros((8, 128), F32)]
    filter_segment(spec, weight_ref, third_ref, twist, bank, out_ref, 0, v_ref, norms)
    row = lax.broadcasted_iota(jnp.int32, (16, 128), 0)
    tail = jnp.zeros((16, 128), F32)
    for slot in range(2):
        left = jnp.broadcast_to(norms[slot].sum(axis=0, keepdims=True), (16, 128))
        for piece in range(3):
            rounded = left.astype(BF).astype(F32)
            tail = jnp.where(row == 3 * slot + piece, rounded, tail)
            left = left - rounded
    for dest in range(8):
        out_ref[dest, 512:528, :] = tail.astype(BF)


def other_kernel(spec, weight_ref, third_ref, twist, bank, half_ref, out_ref, v_ref):
    out_ref[:, :528, :] = half_ref[...]
    filter_segment(spec, weight_ref, third_ref, twist, bank, out_ref, 528, v_ref, None)


def last_kernel(in_ref, table_ref, out_any, out_ref, sems):
    total = jnp.zeros((16, 128), F32)
    for s in range(8):
        total = total + in_ref[s, 512:528, :].astype(F32)
    row = lax.broadcasted_iota(jnp.int32, (16, 128), 0)
    scales = []
    for slot in range(2):
        mine = (row >= 3 * slot) & (row < 3 * slot + 3)
        sigma2 = jnp.sum(jnp.where(mine, total, 0.0), axis=(0, 1), keepdims=True)
        scales.append(1.0 / jnp.sqrt(NSAMP * sigma2))
    _, _, core = place()
    copies = []
    for pair in range(4):
        other, slot = pair // 2, pair % 2
        seg = (core + other) % 2
        at = 528 * other + 256 * slot
        parts = []
        for r in range(4):
            both = jnp.concatenate([in_ref[2 * r, at : at + 256, :], in_ref[2 * r + 1, at : at + 256, :]], axis=1)
            both = both.astype(F32)
            parts.append((both[:128], both[128:]))
        outs = four_way(1, parts)
        for p, (re, im) in enumerate(outs):
            right = jnp.concatenate([re, im], axis=0)
            hi = right.astype(BF)
            lo = (right - hi.astype(F32)).astype(BF)
            cos = dot_nt(table_ref[p, 0], hi) + dot_nt(table_ref[p, 0], lo)
            sin = dot_nt(table_ref[p, 1], hi) + dot_nt(table_ref[p, 1], lo)
            sr = cos[:, :128] - sin[:, 128:]
            si = sin[:, :128] + cos[:, 128:]
            out_ref[pair, pl.ds(p, 256, stride=4), :] = jnp.sqrt(sr * sr + si * si) * scales[slot]
        copies.append(pltpu.make_async_copy(out_ref.at[pair], out_any.at[seg, slot], sems.at[pair]))
        copies[pair].start()
    for copy in copies:
        copy.wait()


def call(kernel, ins, outs, specs, flops, moved, scratch=(), limit=16, space=VMEM):
    return pl.pallas_call(
        kernel,
        out_shape=outs,
        in_specs=specs,
        out_specs=space if isinstance(space, tuple) else jax.tree.map(lambda _: space, outs),
        scratch_shapes=list(scratch),
        compiler_params=pltpu.CompilerParams(vmem_limit_bytes=limit * MIB),
        cost_estimate=pl.CostEstimate(flops=flops, bytes_accessed=moved, transcendentals=0),
    )(*ins)


def shape(*dims, dtype=BF):
    return jax.ShapeDtypeStruct(dims, dtype)


def per_device(strain, gate_start, gate_span, asd, bank, assign):
    const = {name: jnp.asarray(value) for name, value in tables().items()}
    swap_core = [(i, i ^ 1) for i in range(16)]

    blk = (2, 2, 4, 16, 128)
    gated, weight, twist, *picked = call(
        gate_kernel, (strain, gate_start, gate_span, assign, bank, asd, const["back"], const["shift"]),
        (
            shape(8, 128, 128), shape(4, 256, 128, dtype=F32), shape(2, 1024, 128, dtype=F32),
            *[shape(2, *blk)] * 8,
        ),
        [ANY] * 8, 10**8, 4 * MIB,
        [
            pltpu.VMEM((128, 1024), F32), pltpu.VMEM((2, 32, 64, 128), F32), pltpu.SMEM((2, 1, 2), jnp.int32),
            pltpu.SMEM((2, 1, 2), jnp.int32), pltpu.SMEM((32,), jnp.int32), pltpu.VMEM((1024, 128), F32),
            pltpu.VMEM((2, 1024, 128), F32), pltpu.VMEM((2, 1024, 128), F32), pltpu.SemaphoreType.DMA((8,)),
        ],
        limit=63,
    )
    columns = lax.all_to_all(gated, "seg", 0, 0)

    pieces = picked[:1]
    for (rz, rx), send in zip(OFFSETS[1:], picked[1:]):
        hop = [(i, (i // 4 + rx) % 4 * 4 + i % 4 ^ 2 * rz) for i in range(16)]
        pieces.append(lax.ppermute(send, "tmpl", hop))
    turned, token = call(
        first_kernel, (columns, const["first"], *pieces[1:4]), (shape(8, 2, 4, 32, 128), shape(8, 128, dtype=F32)),
        [VMEM] * 2 + [ANY] * 3, 3 * 10**8, 4 * MIB, [pltpu.VMEM((512, 512), F32)],
    )
    crosses = call(
        pack_kernel, (*pieces, token), (shape(2, *blk),) * 4, [ANY] * 9, 1, MIB, [pltpu.SemaphoreType.DMA((8,))],
        limit=8, space=(ANY,) * 4,
    )
    crossed = [lax.ppermute(cross, "tmpl", swap_core) for cross in crosses]
    ordered = call(
        assemble_kernel, (*pieces, *crossed), shape(16, *blk), [ANY] * 12, 1, 10 * MIB,
        [pltpu.SemaphoreType.DMA((16,))], limit=8,
    )
    own = lax.all_to_all(turned, "seg", 0, 0)
    spec = call(
        second_kernel, (own, const["second"], ordered), shape(2, 1024, 128, dtype=F32),
        [VMEM] * 2 + [ANY], 1, 1, [pltpu.VMEM((4, 256, 256), F32)],
    )
    other_spec = lax.ppermute(spec, "tmpl", swap_core)
    half = call(
        own_kernel,
        (spec, weight, const["third"], twist, ordered),
        shape(8, 528, 128), [VMEM] * 5, 2 * 10**9, 10 * MIB, [pltpu.VMEM((4, 2, 256, 256), F32)],
    )
    inner = call(
        other_kernel,
        (other_spec, weight, const["third"], twist, ordered, half),
        shape(8, 1040, 128), [VMEM] * 6, 2 * 10**9, 10 * MIB, [pltpu.VMEM((4, 2, 256, 256), F32)],
    )
    series = lax.all_to_all(inner, "seg", 0, 0)
    return call(
        last_kernel, (series, const["last"]), shape(2, 2, 1024, 128, dtype=F32), [VMEM] * 2, 3 * 10**9, 6 * MIB,
        [pltpu.VMEM((4, 1024, 128), F32), pltpu.SemaphoreType.DMA((4,))], space=ANY,
    )


def solution(mesh):
    placed = (
        P(None, "seg", None),
        P(None, "seg", None),
        P(None, "seg", None),
        P(None, "seg"),
        P(None, None, "tmpl", "seg"),
        P(),
    )
    return jax.shard_map(
        per_device,
        mesh=mesh,
        in_specs=placed,
        out_specs=P(None, "tmpl", None, "seg"),
        check_vma=False,
    )
```

```python
import functools
import math

import jax
import jax.numpy as jnp
import numpy as np
from jax import lax
from jax.experimental import pallas as pl
from jax.experimental.pallas import tpu as pltpu
from jax.sharding import PartitionSpec as P

BF = jnp.bfloat16
F32 = jnp.float32
NSAMP = 1048576
VMEM = pl.BlockSpec(memory_space=pltpu.VMEM)
SMEM = pl.BlockSpec(memory_space=pltpu.SMEM)
ANY = pl.BlockSpec(memory_space=pl.ANY)
MIB = 1 << 20
OFFSETS = [(0, 0), (1, 0), (1, 2), (0, 2), (1, 1), (1, 3), (0, 1), (0, 3)]


def phases(product, count):
    angle = 2.0 * math.pi / count * (product % count).astype(np.float64)
    return np.cos(angle), np.sin(angle)


def split_hi_lo(table):
    table = table.astype(np.float32)
    hi = table.astype(jnp.bfloat16)
    lo = (table - hi.astype(np.float32)).astype(jnp.bfloat16)
    return hi, lo


@functools.cache
def tables():
    q = np.arange(256)
    c, s = phases(q[:, None] * q[None, :], 256)
    hi, lo = split_hi_lo(np.concatenate([c, -s], axis=1))
    first = np.concatenate([hi, lo], axis=1).astype(np.float32)
    k2 = np.arange(1024)
    rows = np.concatenate([4 * np.arange(32), 128 * np.arange(8), np.arange(8), 1024 * np.arange(8)])
    c, s = phases(rows[:, None] * k2[None, :], NSAMP)
    turn = np.concatenate([c, -s]).astype(np.float32)
    first = np.concatenate([first, turn], axis=0)
    c, s = phases(q[:, None] * q[None, :], 256)
    (ch, cl), (sh, sl) = split_hi_lo(c), split_hi_lo(s)
    second = np.concatenate([ch, sh, cl, sl], axis=1)
    c, s = phases(q[:, None] * np.arange(4)[None, :], 1024)
    lag = np.zeros((256, 128), np.float32)
    lag[:, 0:8:2], lag[:, 1:8:2] = c, -s
    second = np.concatenate([second.astype(np.float32), lag], axis=1)
    third = []
    for p in range(4):
        c, s = phases(q[:, None] * (4 * q[None, :] + p), 1024)
        c, s = c.astype(np.float32), s.astype(np.float32)
        third.append(np.concatenate([c, s], 1))
    n1 = np.arange(1024)
    c, s = phases(n1[:, None] * np.arange(128)[None, :], NSAMP)
    back = np.stack([c, s]).astype(np.float32)
    c, s = phases(n1[:, None] * 128 * np.arange(128)[None, :], NSAMP)
    shift = np.stack([c, s]).astype(np.float32)
    last = []
    for p in range(4):
        c, s = phases((4 * q[:, None] + p) * q[None, :], 1024)
        last.append(np.stack([c, s]).astype(np.float32))
    return dict(
        first=first,
        second=second,
        third=np.stack(third).astype(jnp.bfloat16),
        back=back,
        shift=shift,
        last=np.stack(last).astype(jnp.bfloat16),
    )


def dot(a, b):
    return jnp.dot(a, b, preferred_element_type=F32)


def dot_nt(a, b):
    return lax.dot_general(a, b, (((1,), (1,)), ((), ())), preferred_element_type=F32)


def place():
    t = lax.axis_index("tmpl")
    return t // 4, (t // 2) % 2, t % 2


def gate_kernel(
    strain_ref, start_any, span_any, assign_any, bank_any, asd_any, back_any, shift_any,
    out_ref, weight_ref, twist_ref, *rest
):
    pick_refs, rest = rest[:8], rest[8:]
    strain, bank_ref, start_ref, span_ref, assign_ref, asd_ref, back_ref, shift_ref, sems = rest
    x, z, core = place()
    copies = [
        pltpu.make_async_copy(start_any, start_ref, sems.at[0]),
        pltpu.make_async_copy(span_any, span_ref, sems.at[1]),
        pltpu.make_async_copy(strain_ref.at[core], strain, sems.at[2]),
        pltpu.make_async_copy(assign_any, assign_ref, sems.at[3]),
        pltpu.make_async_copy(bank_any, bank_ref, sems.at[4]),
        pltpu.make_async_copy(asd_any, asd_ref, sems.at[5]),
        pltpu.make_async_copy(back_any, back_ref, sems.at[6]),
        pltpu.make_async_copy(shift_any, shift_ref, sems.at[7]),
    ]
    for copy in copies:
        copy.start()
    row = lax.broadcasted_iota(jnp.int32, (128, 128), 0)
    lane = lax.broadcasted_iota(jnp.int32, (128, 128), 1)
    order = jnp.where(lane == row % 32 * 4 + row // 32, 1.0, 0.0).astype(BF)
    pick = jnp.where(row == lane % 32 * 4 + lane // 32, 1.0, 0.0).astype(BF)
    for copy in copies[:3]:
        copy.wait()
    blocks = []
    for dest in range(8):
        value = strain[:, 128 * dest : 128 * dest + 128]
        sample = row * 1024 + (lane + 128 * dest)
        for g in range(2):
            first = start_ref[core, 0, g]
            inside = (sample >= first) & (sample < first + span_ref[core, 0, g])
            value = jnp.where(inside, 0.0, value)
        blocks.append(value.astype(BF))
    picked = dot(jnp.concatenate(blocks, axis=0), pick).astype(BF)
    wide = jnp.concatenate([picked[128 * dest : 128 * dest + 128] for dest in range(8)], axis=1)
    ordered = dot(order, wide).astype(BF)
    for dest in range(8):
        out_ref[dest] = ordered[:, 128 * dest : 128 * dest + 128]

    for copy in copies[3:5]:
        copy.wait()
    for i in range(16):
        (rz, rx), rc = OFFSETS[i // 2], i % 2
        dest = ((x + rx) % 4) * 4 + (z + rz) % 2 * 2 + (core + rc) % 2
        for slot in range(2):
            chosen = assign_ref[2 * dest + slot]
            for part in range(2):
                for p in range(4):
                    value = bank_ref[part, chosen, pl.ds(p, 16, stride=4), :].astype(BF)
                    pick_refs[i // 2][rc, slot, part, p] = value

    for copy in copies[5:]:
        copy.wait()
    for p in range(4):
        asd = asd_ref[pl.ds(p, 256, stride=4), :]
        weight_ref[p] = 1.0 / (asd * asd)
    own = lane == lax.axis_index("seg")
    for i in range(8):
        rows = slice(128 * i, 128 * i + 128)
        shift = [jnp.sum(jnp.where(own, shift_ref[part, rows, :], 0.0), axis=1, keepdims=True) for part in range(2)]
        re, im = back_ref[0, rows, :], back_ref[1, rows, :]
        twist_ref[0, rows, :] = re * shift[0] - im * shift[1]
        twist_ref[1, rows, :] = re * shift[1] + im * shift[0]


def pack_kernel(*refs):
    piece_refs, out_refs, sems = refs[:8], refs[9:11], refs[11]
    copies = [pltpu.make_async_copy(piece_refs[i].at[1], out_refs[i // 4].at[i % 4], sems.at[i]) for i in range(8)]
    for copy in copies:
        copy.start()
    for copy in copies:
        copy.wait()


def four_way(sign, parts):
    (ar, ai), (br, bi), (cr, ci), (dr, di) = parts
    sr, si = ar + cr, ai + ci
    tr, ti = ar - cr, ai - ci
    ur, ui = br + dr, bi + di
    vr, vi = br - dr, bi - di
    if sign > 0:
        wr, wi = -vi, vr
    else:
        wr, wi = vi, -vr
    return ((sr + ur, si + ui), (tr + wr, ti + wi), (sr - ur, si - ui), (tr - wr, ti - wi))


def first_kernel(cols_ref, table_ref, *refs):
    out_ref, token_ref, z_ref = refs[-3:]
    token_ref[...] = jnp.zeros_like(token_ref)
    turn_ref = table_ref.at[256:368].reshape(2, 56, 1024)
    turned = jnp.concatenate([cols_ref[:, 32 * r : 32 * r + 32, :].reshape(256, 128).T for r in range(4)], axis=0)
    z_ref[...] = dot(turned, table_ref[:256, :512].astype(BF)) + dot(turned, table_ref[:256, 512:].astype(BF))
    seg = 32 + lax.axis_index("seg")
    seg_re, seg_im = turn_ref[0, pl.ds(seg, 1), :], turn_ref[1, pl.ds(seg, 1), :]
    for r1 in range(4):
        low_re, low_im = turn_ref[0, 40 + r1 : 41 + r1, :], turn_ref[1, 40 + r1 : 41 + r1, :]
        base_re = low_re * seg_re - low_im * seg_im
        base_im = low_re * seg_im + low_im * seg_re
        for i in range(2):
            at = slice(16 * i, 16 * i + 16)
            rows = slice(32 * r1 + 16 * i, 32 * r1 + 16 * i + 16)
            fr, fi = turn_ref[0, at, :], turn_ref[1, at, :]
            tr = fr * base_re - fi * base_im
            ti = fr * base_im + fi * base_re
            sums = []
            for r in range(4):
                here = slice(128 * r + rows.start, 128 * r + rows.stop)
                re, im = z_ref[here, :256], z_ref[here, 256:]
                if r > 0:
                    pr, pi = turn_ref[0, 48 + r : 49 + r, :256], turn_ref[1, 48 + r : 49 + r, :256]
                    re, im = re * pr - im * pi, re * pi + im * pr
                sums.append((re, im))
            outs = four_way(-1, sums)
            for k, (re, im) in enumerate(outs):
                wr, wi = tr[:, 256 * k : 256 * k + 256], ti[:, 256 * k : 256 * k + 256]
                done = ((re * wr - im * wi).astype(BF), (re * wi + im * wr).astype(BF))
                for half in range(2):
                    for part in range(2):
                        out_ref[2 * k + half, part, r1, at] = done[part][:, 128 * half : 128 * half + 128]


def second_kernel(own_ref, table_ref, after_ref, spec_ref, z_ref):
    del after_ref
    hi, lo = table_ref[:, :512].astype(BF), table_ref[:, 512:1024].astype(BF)
    for r in range(4):
        re = own_ref[:, 0, r].reshape(256, 128)
        im = own_ref[:, 1, r].reshape(256, 128)
        right = jnp.concatenate([jnp.concatenate([re, im], axis=1), jnp.concatenate([im, -re], axis=1)], axis=0)
        z_ref[r] = dot(hi, right) + dot(lo, right)
    for i in range(8):
        rows = slice(32 * i, 32 * i + 32)
        sums = [(z_ref[0, rows, :128], z_ref[0, rows, 128:])]
        for r in range(1, 4):
            at = 1024 + 2 * r
            pr, pi = table_ref[rows, at : at + 1], table_ref[rows, at + 1 : at + 2]
            re, im = z_ref[r, rows, :128], z_ref[r, rows, 128:]
            sums.append((re * pr - im * pi, re * pi + im * pr))
        for k, parts in enumerate(four_way(-1, sums)):
            for part in range(2):
                spec_ref[part, 256 * k + 32 * i : 256 * k + 32 * i + 32, :] = parts[part]


def assemble_kernel(*refs):
    piece_refs, cross_refs, bank, sems = refs[:8], refs[8:10], *refs[10:]
    x, z, core = place()
    copies = []
    for i, (rz, rx) in enumerate(OFFSETS):
        for rc in range(2):
            src = piece_refs[i].at[0] if rc == 0 else cross_refs[i // 4].at[i % 4]
            origin = ((x + 4 - rx) % 4) * 4 + (z + rz) % 2 * 2 + (core + rc) % 2
            copies.append(pltpu.make_async_copy(src, bank.at[origin], sems.at[len(copies)]))
    for copy in copies:
        copy.start()
    for copy in copies:
        copy.wait()


def filter_segment(spec, weight_ref, third_ref, twist, bank, out_ref, first_row, v_ref, norms):
    for p in range(4):
        weight = weight_ref[p]
        sr = spec[0, pl.ds(p, 256, stride=4), :] * weight
        si = spec[1, pl.ds(p, 256, stride=4), :] * weight
        lanes_re, lanes_im = [], []
        for slot in range(2):
            hr = bank[:, slot, 0, p].reshape(256, 128).astype(F32)
            hi = bank[:, slot, 1, p].reshape(256, 128).astype(F32)
            if norms is not None:
                power = (hr * hr + hi * hi) * weight
                norms[slot] = norms[slot] + power.reshape(32, 8, 128).sum(axis=0)
            lanes_re.append((sr * hr + si * hi).astype(BF))
            lanes_im.append((si * hr - sr * hi).astype(BF))
        re, im = jnp.concatenate(lanes_re, axis=1), jnp.concatenate(lanes_im, axis=1)
        v_ref[p, 0] = dot(third_ref[p], jnp.concatenate([re, -im], axis=0))
        v_ref[p, 1] = dot(third_ref[p], jnp.concatenate([im, re], axis=0))
    for i in range(8):
        rows = slice(32 * i, 32 * i + 32)
        half, inside = i // 4, (i % 4) * 32
        for slot in range(2):
            cols = slice(128 * slot, 128 * slot + 128)
            outs = four_way(1, [(v_ref[p, 0, rows, cols], v_ref[p, 1, rows, cols]) for p in range(4)])
            for k, (re, im) in enumerate(outs):
                wr = twist[0, 256 * k + 32 * i : 256 * k + 32 * i + 32, :]
                wi = twist[1, 256 * k + 32 * i : 256 * k + 32 * i + 32, :]
                at = first_row + slot * 256 + inside
                out_ref[2 * k + half, at : at + 32, :] = (re * wr - im * wi).astype(BF)
                out_ref[2 * k + half, at + 128 : at + 160, :] = (re * wi + im * wr).astype(BF)


def own_kernel(spec, weight_ref, third_ref, twist, bank, out_ref, v_ref):
    norms = [jnp.zeros((8, 128), F32), jnp.zeros((8, 128), F32)]
    filter_segment(spec, weight_ref, third_ref, twist, bank, out_ref, 0, v_ref, norms)
    row = lax.broadcasted_iota(jnp.int32, (16, 128), 0)
    tail = jnp.zeros((16, 128), F32)
    for slot in range(2):
        left = jnp.broadcast_to(norms[slot].sum(axis=0, keepdims=True), (16, 128))
        for piece in range(3):
            rounded = left.astype(BF).astype(F32)
            tail = jnp.where(row == 3 * slot + piece, rounded, tail)
            left = left - rounded
    for dest in range(8):
        out_ref[dest, 512:528, :] = tail.astype(BF)


def other_kernel(spec, weight_ref, third_ref, twist, bank, half_ref, out_ref, v_ref):
    out_ref[:, :528, :] = half_ref[...]
    filter_segment(spec, weight_ref, third_ref, twist, bank, out_ref, 528, v_ref, None)


def last_kernel(in_ref, table_ref, out_any, out_ref, sems):
    total = jnp.zeros((16, 128), F32)
    for s in range(8):
        total = total + in_ref[s, 512:528, :].astype(F32)
    row = lax.broadcasted_iota(jnp.int32, (16, 128), 0)
    scales = []
    for slot in range(2):
        mine = (row >= 3 * slot) & (row < 3 * slot + 3)
        sigma2 = jnp.sum(jnp.where(mine, total, 0.0), axis=(0, 1), keepdims=True)
        scales.append(1.0 / jnp.sqrt(NSAMP * sigma2))
    _, _, core = place()
    copies = []
    for pair in range(4):
        other, slot = pair // 2, pair % 2
        seg = (core + other) % 2
        at = 528 * other + 256 * slot
        parts = []
        for r in range(4):
            both = jnp.concatenate([in_ref[2 * r, at : at + 256, :], in_ref[2 * r + 1, at : at + 256, :]], axis=1)
            both = both.astype(F32)
            parts.append((both[:128], both[128:]))
        outs = four_way(1, parts)
        for p, (re, im) in enumerate(outs):
            right = jnp.concatenate([re, im], axis=0).astype(BF)
            cos = dot_nt(table_ref[p, 0], right)
            sin = dot_nt(table_ref[p, 1], right)
            sr = cos[:, :128] - sin[:, 128:]
            si = sin[:, :128] + cos[:, 128:]
            out_ref[pair, pl.ds(p, 256, stride=4), :] = jnp.sqrt(sr * sr + si * si) * scales[slot]
        copies.append(pltpu.make_async_copy(out_ref.at[pair], out_any.at[seg, slot], sems.at[pair]))
        copies[pair].start()
    for copy in copies:
        copy.wait()


def call(kernel, ins, outs, specs, flops, moved, scratch=(), limit=16, space=VMEM):
    return pl.pallas_call(
        kernel,
        out_shape=outs,
        in_specs=specs,
        out_specs=space if isinstance(space, tuple) else jax.tree.map(lambda _: space, outs),
        scratch_shapes=list(scratch),
        compiler_params=pltpu.CompilerParams(vmem_limit_bytes=limit * MIB),
        cost_estimate=pl.CostEstimate(flops=flops, bytes_accessed=moved, transcendentals=0),
    )(*ins)


def shape(*dims, dtype=BF):
    return jax.ShapeDtypeStruct(dims, dtype)


def per_device(strain, gate_start, gate_span, asd, bank, assign):
    const = {name: jnp.asarray(value) for name, value in tables().items()}
    swap_core = [(i, i ^ 1) for i in range(16)]

    blk = (2, 2, 4, 16, 128)
    gated, weight, twist, *picked = call(
        gate_kernel, (strain, gate_start, gate_span, assign, bank, asd, const["back"], const["shift"]),
        (
            shape(8, 128, 128), shape(4, 256, 128, dtype=F32), shape(2, 1024, 128, dtype=F32),
            *[shape(2, *blk)] * 8,
        ),
        [ANY] * 8, 10**8, 4 * MIB,
        [
            pltpu.VMEM((128, 1024), F32), pltpu.VMEM((2, 32, 64, 128), F32), pltpu.SMEM((2, 1, 2), jnp.int32),
            pltpu.SMEM((2, 1, 2), jnp.int32), pltpu.SMEM((32,), jnp.int32), pltpu.VMEM((1024, 128), F32),
            pltpu.VMEM((2, 1024, 128), F32), pltpu.VMEM((2, 1024, 128), F32), pltpu.SemaphoreType.DMA((8,)),
        ],
        limit=63,
    )
    columns = lax.all_to_all(gated, "seg", 0, 0)

    pieces = picked[:1]
    for (rz, rx), send in zip(OFFSETS[1:], picked[1:]):
        hop = [(i, (i // 4 + rx) % 4 * 4 + i % 4 ^ 2 * rz) for i in range(16)]
        pieces.append(lax.ppermute(send, "tmpl", hop))
    turned, token = call(
        first_kernel, (columns, const["first"], *pieces[1:4]), (shape(8, 2, 4, 32, 128), shape(8, 128, dtype=F32)),
        [VMEM] * 2 + [ANY] * 3, 3 * 10**8, 4 * MIB, [pltpu.VMEM((512, 512), F32)],
    )
    crosses = call(
        pack_kernel, (*pieces, token), (shape(4, *blk),) * 2, [ANY] * 9, 1, MIB, [pltpu.SemaphoreType.DMA((8,))],
        limit=8, space=(ANY,) * 2,
    )
    crossed = [lax.ppermute(cross, "tmpl", swap_core) for cross in crosses]
    ordered = call(
        assemble_kernel, (*pieces, *crossed), shape(16, *blk), [ANY] * 10, 1, 10 * MIB,
        [pltpu.SemaphoreType.DMA((16,))], limit=8,
    )
    own = lax.all_to_all(turned, "seg", 0, 0)
    spec = call(
        second_kernel, (own, const["second"], ordered), shape(2, 1024, 128, dtype=F32),
        [VMEM] * 2 + [ANY], 1, 1, [pltpu.VMEM((4, 256, 256), F32)],
    )
    other_spec = lax.ppermute(spec, "tmpl", swap_core)
    half = call(
        own_kernel,
        (spec, weight, const["third"], twist, ordered),
        shape(8, 528, 128), [VMEM] * 5, 2 * 10**9, 10 * MIB, [pltpu.VMEM((4, 2, 256, 256), F32)],
    )
    inner = call(
        other_kernel,
        (other_spec, weight, const["third"], twist, ordered, half),
        shape(8, 1040, 128), [VMEM] * 6, 2 * 10**9, 10 * MIB, [pltpu.VMEM((4, 2, 256, 256), F32)],
    )
    series = lax.all_to_all(inner, "seg", 0, 0)
    return call(
        last_kernel, (series, const["last"]), shape(2, 2, 1024, 128, dtype=F32), [VMEM] * 2, 3 * 10**9, 6 * MIB,
        [pltpu.VMEM((4, 1024, 128), F32), pltpu.SemaphoreType.DMA((4,))], space=ANY,
    )


def solution(mesh):
    placed = (
        P(None, "seg", None),
        P(None, "seg", None),
        P(None, "seg", None),
        P(None, "seg"),
        P(None, None, "tmpl", "seg"),
        P(),
    )
    return jax.shard_map(
        per_device,
        mesh=mesh,
        in_specs=placed,
        out_specs=P(None, "tmpl", None, "seg"),
        check_vma=False,
    )
```

```python
import functools
import math

import jax
import jax.numpy as jnp
import numpy as np
from jax import lax
from jax.experimental import pallas as pl
from jax.experimental.pallas import tpu as pltpu
from jax.sharding import PartitionSpec as P

BF = jnp.bfloat16
F32 = jnp.float32
NSAMP = 1048576
VMEM = pl.BlockSpec(memory_space=pltpu.VMEM)
SMEM = pl.BlockSpec(memory_space=pltpu.SMEM)
ANY = pl.BlockSpec(memory_space=pl.ANY)
MIB = 1 << 20
OFFSETS = [(0, 0), (1, 0), (1, 2), (0, 2), (1, 1), (1, 3), (0, 1), (0, 3)]


def phases(product, count):
    angle = 2.0 * math.pi / count * (product % count).astype(np.float64)
    return np.cos(angle), np.sin(angle)


def split_hi_lo(table):
    table = table.astype(np.float32)
    hi = table.astype(jnp.bfloat16)
    lo = (table - hi.astype(np.float32)).astype(jnp.bfloat16)
    return hi, lo


@functools.cache
def tables():
    q = np.arange(256)
    c, s = phases(q[:, None] * q[None, :], 256)
    hi, lo = split_hi_lo(np.concatenate([c, -s], axis=1))
    first = np.concatenate([hi, lo], axis=1).astype(np.float32)
    k2 = np.arange(1024)
    rows = np.concatenate([4 * np.arange(32), 128 * np.arange(8), np.arange(8), 1024 * np.arange(8)])
    c, s = phases(rows[:, None] * k2[None, :], NSAMP)
    turn = np.concatenate([c, -s]).astype(np.float32)
    first = np.concatenate([first, turn], axis=0)
    c, s = phases(q[:, None] * q[None, :], 256)
    (ch, cl), (sh, sl) = split_hi_lo(c), split_hi_lo(s)
    second = np.concatenate([ch, sh, cl, sl], axis=1)
    c, s = phases(q[:, None] * np.arange(4)[None, :], 1024)
    lag = np.zeros((256, 128), np.float32)
    lag[:, 0:8:2], lag[:, 1:8:2] = c, -s
    second = np.concatenate([second.astype(np.float32), lag], axis=1)
    third = []
    for p in range(4):
        c, s = phases(q[:, None] * (4 * q[None, :] + p), 1024)
        c, s = c.astype(np.float32), s.astype(np.float32)
        third.append(np.concatenate([c, s], 1))
    n1 = np.arange(1024)
    c, s = phases(n1[:, None] * np.arange(128)[None, :], NSAMP)
    back = np.stack([c, s]).astype(np.float32)
    c, s = phases(n1[:, None] * 128 * np.arange(128)[None, :], NSAMP)
    shift = np.stack([c, s]).astype(np.float32)
    last = []
    for p in range(4):
        c, s = phases((4 * q[:, None] + p) * q[None, :], 1024)
        last.append(np.stack([c, s]).astype(np.float32))
    return dict(
        first=first,
        second=second,
        third=np.stack(third).astype(jnp.bfloat16),
        back=back,
        shift=shift,
        last=np.stack(last).astype(jnp.bfloat16),
    )


def dot(a, b):
    return jnp.dot(a, b, preferred_element_type=F32)


def dot_nt(a, b):
    return lax.dot_general(a, b, (((1,), (1,)), ((), ())), preferred_element_type=F32)


def place():
    t = lax.axis_index("tmpl")
    return t // 4, (t // 2) % 2, t % 2


def gate_kernel(
    strain_ref, start_any, span_any, assign_any, bank_any, asd_any, back_any, shift_any,
    out_ref, weight_ref, twist_ref, *rest
):
    pick_refs, rest = rest[:8], rest[8:]
    strain, bank_ref, start_ref, span_ref, assign_ref, asd_ref, back_ref, shift_ref, sems = rest
    x, z, core = place()
    copies = [
        pltpu.make_async_copy(start_any, start_ref, sems.at[0]),
        pltpu.make_async_copy(span_any, span_ref, sems.at[1]),
        pltpu.make_async_copy(strain_ref.at[core], strain, sems.at[2]),
        pltpu.make_async_copy(assign_any, assign_ref, sems.at[3]),
        pltpu.make_async_copy(bank_any, bank_ref, sems.at[4]),
        pltpu.make_async_copy(asd_any, asd_ref, sems.at[5]),
        pltpu.make_async_copy(back_any, back_ref, sems.at[6]),
        pltpu.make_async_copy(shift_any, shift_ref, sems.at[7]),
    ]
    for copy in copies:
        copy.start()
    row = lax.broadcasted_iota(jnp.int32, (128, 128), 0)
    lane = lax.broadcasted_iota(jnp.int32, (128, 128), 1)
    order = jnp.where(lane == row % 32 * 4 + row // 32, 1.0, 0.0).astype(BF)
    pick = jnp.where(row == lane % 32 * 4 + lane // 32, 1.0, 0.0).astype(BF)
    for copy in copies[:3]:
        copy.wait()
    blocks = []
    for dest in range(8):
        value = strain[:, 128 * dest : 128 * dest + 128]
        sample = row * 1024 + (lane + 128 * dest)
        for g in range(2):
            first = start_ref[core, 0, g]
            inside = (sample >= first) & (sample < first + span_ref[core, 0, g])
            value = jnp.where(inside, 0.0, value)
        blocks.append(value.astype(BF))
    picked = dot(jnp.concatenate(blocks, axis=0), pick).astype(BF)
    wide = jnp.concatenate([picked[128 * dest : 128 * dest + 128] for dest in range(8)], axis=1)
    ordered = dot(order, wide).astype(BF)
    for dest in range(8):
        out_ref[dest] = ordered[:, 128 * dest : 128 * dest + 128]

    for copy in copies[3:5]:
        copy.wait()
    for i in range(16):
        (rz, rx), rc = OFFSETS[i // 2], i % 2
        dest = ((x + rx) % 4) * 4 + (z + rz) % 2 * 2 + (core + rc) % 2
        for slot in range(2):
            chosen = assign_ref[2 * dest + slot]
            for part in range(2):
                for p in range(4):
                    value = bank_ref[part, chosen, pl.ds(p, 16, stride=4), :].astype(BF)
                    pick_refs[i // 2][rc, slot, part, p] = value

    for copy in copies[5:]:
        copy.wait()
    for p in range(4):
        asd = asd_ref[pl.ds(p, 256, stride=4), :]
        weight_ref[p] = 1.0 / (asd * asd)
    own = lane == lax.axis_index("seg")
    for i in range(8):
        rows = slice(128 * i, 128 * i + 128)
        shift = [jnp.sum(jnp.where(own, shift_ref[part, rows, :], 0.0), axis=1, keepdims=True) for part in range(2)]
        re, im = back_ref[0, rows, :], back_ref[1, rows, :]
        twist_ref[0, rows, :] = re * shift[0] - im * shift[1]
        twist_ref[1, rows, :] = re * shift[1] + im * shift[0]


def pack_kernel(*refs):
    piece_refs, out_refs, sems = refs[:8], refs[9:11], refs[11]
    copies = [pltpu.make_async_copy(piece_refs[i].at[1], out_refs[i // 4].at[i % 4], sems.at[i]) for i in range(8)]
    for copy in copies:
        copy.start()
    for copy in copies:
        copy.wait()


def four_way(sign, parts):
    (ar, ai), (br, bi), (cr, ci), (dr, di) = parts
    sr, si = ar + cr, ai + ci
    tr, ti = ar - cr, ai - ci
    ur, ui = br + dr, bi + di
    vr, vi = br - dr, bi - di
    if sign > 0:
        wr, wi = -vi, vr
    else:
        wr, wi = vi, -vr
    return ((sr + ur, si + ui), (tr + wr, ti + wi), (sr - ur, si - ui), (tr - wr, ti - wi))


def first_kernel(cols_ref, table_ref, *refs):
    out_ref, token_ref, z_ref = refs[-3:]
    token_ref[...] = jnp.zeros_like(token_ref)
    turn_ref = table_ref.at[256:368].reshape(2, 56, 1024)
    turned = jnp.concatenate([cols_ref[:, 32 * r : 32 * r + 32, :].reshape(256, 128).T for r in range(4)], axis=0)
    z_ref[...] = dot(turned, table_ref[:256, :512].astype(BF)) + dot(turned, table_ref[:256, 512:].astype(BF))
    seg = 32 + lax.axis_index("seg")
    seg_re, seg_im = turn_ref[0, pl.ds(seg, 1), :], turn_ref[1, pl.ds(seg, 1), :]
    for r1 in range(4):
        low_re, low_im = turn_ref[0, 40 + r1 : 41 + r1, :], turn_ref[1, 40 + r1 : 41 + r1, :]
        base_re = low_re * seg_re - low_im * seg_im
        base_im = low_re * seg_im + low_im * seg_re
        for i in range(2):
            at = slice(16 * i, 16 * i + 16)
            rows = slice(32 * r1 + 16 * i, 32 * r1 + 16 * i + 16)
            fr, fi = turn_ref[0, at, :], turn_ref[1, at, :]
            tr = fr * base_re - fi * base_im
            ti = fr * base_im + fi * base_re
            sums = []
            for r in range(4):
                here = slice(128 * r + rows.start, 128 * r + rows.stop)
                re, im = z_ref[here, :256], z_ref[here, 256:]
                if r > 0:
                    pr, pi = turn_ref[0, 48 + r : 49 + r, :256], turn_ref[1, 48 + r : 49 + r, :256]
                    re, im = re * pr - im * pi, re * pi + im * pr
                sums.append((re, im))
            outs = four_way(-1, sums)
            for k, (re, im) in enumerate(outs):
                wr, wi = tr[:, 256 * k : 256 * k + 256], ti[:, 256 * k : 256 * k + 256]
                done = ((re * wr - im * wi).astype(BF), (re * wi + im * wr).astype(BF))
                for half in range(2):
                    for part in range(2):
                        out_ref[2 * k + half, part, r1, at] = done[part][:, 128 * half : 128 * half + 128]


def second_kernel(own_ref, table_ref, after_ref, also_ref, spec_ref, z_ref):
    del after_ref, also_ref
    hi, lo = table_ref[:, :512].astype(BF), table_ref[:, 512:1024].astype(BF)
    for r in range(4):
        re = own_ref[:, 0, r].reshape(256, 128)
        im = own_ref[:, 1, r].reshape(256, 128)
        right = jnp.concatenate([jnp.concatenate([re, im], axis=1), jnp.concatenate([im, -re], axis=1)], axis=0)
        z_ref[r] = dot(hi, right) + dot(lo, right)
    for i in range(8):
        rows = slice(32 * i, 32 * i + 32)
        sums = [(z_ref[0, rows, :128], z_ref[0, rows, 128:])]
        for r in range(1, 4):
            at = 1024 + 2 * r
            pr, pi = table_ref[rows, at : at + 1], table_ref[rows, at + 1 : at + 2]
            re, im = z_ref[r, rows, :128], z_ref[r, rows, 128:]
            sums.append((re * pr - im * pi, re * pi + im * pr))
        for k, parts in enumerate(four_way(-1, sums)):
            for part in range(2):
                spec_ref[part, 256 * k + 32 * i : 256 * k + 32 * i + 32, :] = parts[part]


def assemble_kernel(*refs):
    piece_refs, cross_refs, bank, sems = refs[:8], refs[8:10], *refs[10:]
    x, z, core = place()
    copies = []
    for i, (rz, rx) in enumerate(OFFSETS):
        for rc in range(2):
            src = piece_refs[i].at[0] if rc == 0 else cross_refs[i // 4].at[i % 4]
            origin = ((x + 4 - rx) % 4) * 4 + (z + rz) % 2 * 2 + (core + rc) % 2
            copies.append(pltpu.make_async_copy(src, bank.at[origin], sems.at[len(copies)]))
    for copy in copies:
        copy.start()
    for copy in copies:
        copy.wait()


def filter_segment(spec, weight_ref, third_ref, twist, bank, out_ref, first_row, v_ref, norms):
    for p in range(4):
        weight = weight_ref[p]
        sr = spec[0, pl.ds(p, 256, stride=4), :] * weight
        si = spec[1, pl.ds(p, 256, stride=4), :] * weight
        lanes_re, lanes_im = [], []
        for slot in range(2):
            hr = bank[:, slot, 0, p].reshape(256, 128).astype(F32)
            hi = bank[:, slot, 1, p].reshape(256, 128).astype(F32)
            if norms is not None:
                power = (hr * hr + hi * hi) * weight
                norms[slot] = norms[slot] + power.reshape(32, 8, 128).sum(axis=0)
            lanes_re.append((sr * hr + si * hi).astype(BF))
            lanes_im.append((si * hr - sr * hi).astype(BF))
        re, im = jnp.concatenate(lanes_re, axis=1), jnp.concatenate(lanes_im, axis=1)
        v_ref[p, 0] = dot(third_ref[p], jnp.concatenate([re, -im], axis=0))
        v_ref[p, 1] = dot(third_ref[p], jnp.concatenate([im, re], axis=0))
    for i in range(8):
        rows = slice(32 * i, 32 * i + 32)
        half, inside = i // 4, (i % 4) * 32
        for slot in range(2):
            cols = slice(128 * slot, 128 * slot + 128)
            outs = four_way(1, [(v_ref[p, 0, rows, cols], v_ref[p, 1, rows, cols]) for p in range(4)])
            for k, (re, im) in enumerate(outs):
                wr = twist[0, 256 * k + 32 * i : 256 * k + 32 * i + 32, :]
                wi = twist[1, 256 * k + 32 * i : 256 * k + 32 * i + 32, :]
                at = first_row + slot * 256 + inside
                out_ref[2 * k + half, at : at + 32, :] = (re * wr - im * wi).astype(BF)
                out_ref[2 * k + half, at + 128 : at + 160, :] = (re * wi + im * wr).astype(BF)


def own_kernel(spec, weight_ref, third_ref, twist, bank, out_ref, v_ref):
    norms = [jnp.zeros((8, 128), F32), jnp.zeros((8, 128), F32)]
    filter_segment(spec, weight_ref, third_ref, twist, bank, out_ref, 0, v_ref, norms)
    row = lax.broadcasted_iota(jnp.int32, (16, 128), 0)
    tail = jnp.zeros((16, 128), F32)
    for slot in range(2):
        left = jnp.broadcast_to(norms[slot].sum(axis=0, keepdims=True), (16, 128))
        for piece in range(3):
            rounded = left.astype(BF).astype(F32)
            tail = jnp.where(row == 3 * slot + piece, rounded, tail)
            left = left - rounded
    for dest in range(8):
        out_ref[dest, 512:528, :] = tail.astype(BF)


def other_kernel(spec, weight_ref, third_ref, twist, bank, half_ref, out_ref, v_ref):
    out_ref[:, :528, :] = half_ref[...]
    filter_segment(spec, weight_ref, third_ref, twist, bank, out_ref, 528, v_ref, None)


def last_kernel(in_ref, table_ref, out_any, out_ref, sems):
    total = jnp.zeros((16, 128), F32)
    for s in range(8):
        total = total + in_ref[s, 512:528, :].astype(F32)
    row = lax.broadcasted_iota(jnp.int32, (16, 128), 0)
    scales = []
    for slot in range(2):
        mine = (row >= 3 * slot) & (row < 3 * slot + 3)
        sigma2 = jnp.sum(jnp.where(mine, total, 0.0), axis=(0, 1), keepdims=True)
        scales.append(1.0 / jnp.sqrt(NSAMP * sigma2))
    _, _, core = place()
    copies = []
    for pair in range(4):
        other, slot = pair // 2, pair % 2
        seg = (core + other) % 2
        at = 528 * other + 256 * slot
        parts = []
        for r in range(4):
            both = jnp.concatenate([in_ref[2 * r, at : at + 256, :], in_ref[2 * r + 1, at : at + 256, :]], axis=1)
            both = both.astype(F32)
            parts.append((both[:128], both[128:]))
        outs = four_way(1, parts)
        for p, (re, im) in enumerate(outs):
            right = jnp.concatenate([re, im], axis=0).astype(BF)
            cos = dot_nt(table_ref[p, 0], right)
            sin = dot_nt(table_ref[p, 1], right)
            sr = cos[:, :128] - sin[:, 128:]
            si = sin[:, :128] + cos[:, 128:]
            out_ref[pair, pl.ds(p, 256, stride=4), :] = jnp.sqrt(sr * sr + si * si) * scales[slot]
        copies.append(pltpu.make_async_copy(out_ref.at[pair], out_any.at[seg, slot], sems.at[pair]))
        copies[pair].start()
    for copy in copies:
        copy.wait()


def call(kernel, ins, outs, specs, flops, moved, scratch=(), limit=16, space=VMEM):
    return pl.pallas_call(
        kernel,
        out_shape=outs,
        in_specs=specs,
        out_specs=space if isinstance(space, tuple) else jax.tree.map(lambda _: space, outs),
        scratch_shapes=list(scratch),
        compiler_params=pltpu.CompilerParams(vmem_limit_bytes=limit * MIB),
        cost_estimate=pl.CostEstimate(flops=flops, bytes_accessed=moved, transcendentals=0),
    )(*ins)


def shape(*dims, dtype=BF):
    return jax.ShapeDtypeStruct(dims, dtype)


def per_device(strain, gate_start, gate_span, asd, bank, assign):
    const = {name: jnp.asarray(value) for name, value in tables().items()}
    swap_core = [(i, i ^ 1) for i in range(16)]

    blk = (2, 2, 4, 16, 128)
    gated, weight, twist, *picked = call(
        gate_kernel, (strain, gate_start, gate_span, assign, bank, asd, const["back"], const["shift"]),
        (
            shape(8, 128, 128), shape(4, 256, 128, dtype=F32), shape(2, 1024, 128, dtype=F32),
            *[shape(2, *blk)] * 8,
        ),
        [ANY] * 8, 10**8, 4 * MIB,
        [
            pltpu.VMEM((128, 1024), F32), pltpu.VMEM((2, 32, 64, 128), F32), pltpu.SMEM((2, 1, 2), jnp.int32),
            pltpu.SMEM((2, 1, 2), jnp.int32), pltpu.SMEM((32,), jnp.int32), pltpu.VMEM((1024, 128), F32),
            pltpu.VMEM((2, 1024, 128), F32), pltpu.VMEM((2, 1024, 128), F32), pltpu.SemaphoreType.DMA((8,)),
        ],
        limit=63,
    )
    columns = lax.all_to_all(gated, "seg", 0, 0)

    pieces = picked[:1]
    for (rz, rx), send in zip(OFFSETS[1:], picked[1:]):
        hop = [(i, (i // 4 + rx) % 4 * 4 + i % 4 ^ 2 * rz) for i in range(16)]
        pieces.append(lax.ppermute(send, "tmpl", hop))
    turned, token = call(
        first_kernel, (columns, const["first"], *pieces[1:4]), (shape(8, 2, 4, 32, 128), shape(8, 128, dtype=F32)),
        [VMEM] * 2 + [ANY] * 3, 3 * 10**8, 4 * MIB, [pltpu.VMEM((512, 512), F32)],
    )
    crosses = call(
        pack_kernel, (*pieces, token), (shape(4, *blk),) * 2, [ANY] * 9, 1, MIB, [pltpu.SemaphoreType.DMA((8,))],
        limit=8, space=(ANY,) * 2,
    )
    crossed = [lax.ppermute(cross, "tmpl", swap_core) for cross in crosses]
    ordered = call(
        assemble_kernel, (*pieces, *crossed), shape(16, *blk), [ANY] * 10, 1, 10 * MIB,
        [pltpu.SemaphoreType.DMA((16,))], limit=8,
    )
    own = lax.all_to_all(turned, "seg", 0, 0)
    spec = call(
        second_kernel, (own, const["second"], *crossed), shape(2, 1024, 128, dtype=F32),
        [VMEM] * 2 + [ANY] * 2, 1, 1, [pltpu.VMEM((4, 256, 256), F32)],
    )
    other_spec = lax.ppermute(spec, "tmpl", swap_core)
    half = call(
        own_kernel,
        (spec, weight, const["third"], twist, ordered),
        shape(8, 528, 128), [VMEM] * 5, 2 * 10**9, 10 * MIB, [pltpu.VMEM((4, 2, 256, 256), F32)],
    )
    inner = call(
        other_kernel,
        (other_spec, weight, const["third"], twist, ordered, half),
        shape(8, 1040, 128), [VMEM] * 6, 2 * 10**9, 10 * MIB, [pltpu.VMEM((4, 2, 256, 256), F32)],
    )
    series = lax.all_to_all(inner, "seg", 0, 0)
    return call(
        last_kernel, (series, const["last"]), shape(2, 2, 1024, 128, dtype=F32), [VMEM] * 2, 3 * 10**9, 6 * MIB,
        [pltpu.VMEM((4, 1024, 128), F32), pltpu.SemaphoreType.DMA((4,))], space=ANY,
    )


def solution(mesh):
    placed = (
        P(None, "seg", None),
        P(None, "seg", None),
        P(None, "seg", None),
        P(None, "seg"),
        P(None, None, "tmpl", "seg"),
        P(),
    )
    return jax.shard_map(
        per_device,
        mesh=mesh,
        in_specs=placed,
        out_specs=P(None, "tmpl", None, "seg"),
        check_vma=False,
    )
```

```python
import functools
import math

import jax
import jax.numpy as jnp
import numpy as np
from jax import lax
from jax.experimental import pallas as pl
from jax.experimental.pallas import tpu as pltpu
from jax.sharding import PartitionSpec as P

BF = jnp.bfloat16
F32 = jnp.float32
NSAMP = 1048576
VMEM = pl.BlockSpec(memory_space=pltpu.VMEM)
SMEM = pl.BlockSpec(memory_space=pltpu.SMEM)
ANY = pl.BlockSpec(memory_space=pl.ANY)
MIB = 1 << 20
OFFSETS = [(0, 0), (1, 0), (1, 2), (0, 2), (1, 1), (1, 3), (0, 1), (0, 3)]


def phases(product, count):
    angle = 2.0 * math.pi / count * (product % count).astype(np.float64)
    return np.cos(angle), np.sin(angle)


def split_hi_lo(table):
    table = table.astype(np.float32)
    hi = table.astype(jnp.bfloat16)
    lo = (table - hi.astype(np.float32)).astype(jnp.bfloat16)
    return hi, lo


@functools.cache
def tables():
    q = np.arange(256)
    c, s = phases(q[:, None] * q[None, :], 256)
    hi, lo = split_hi_lo(np.concatenate([c, -s], axis=1))
    first = np.concatenate([hi, lo], axis=1).astype(np.float32)
    k2 = np.arange(1024)
    rows = np.concatenate([4 * np.arange(32), 128 * np.arange(8), np.arange(8), 1024 * np.arange(8)])
    c, s = phases(rows[:, None] * k2[None, :], NSAMP)
    turn = np.concatenate([c, -s]).astype(np.float32)
    first = np.concatenate([first, turn], axis=0)
    c, s = phases(q[:, None] * q[None, :], 256)
    (ch, cl), (sh, sl) = split_hi_lo(c), split_hi_lo(s)
    second = np.concatenate([ch, sh, cl, sl], axis=1)
    c, s = phases(q[:, None] * np.arange(4)[None, :], 1024)
    lag = np.zeros((256, 128), np.float32)
    lag[:, 0:8:2], lag[:, 1:8:2] = c, -s
    second = np.concatenate([second.astype(np.float32), lag], axis=1)
    third = []
    for p in range(4):
        c, s = phases(q[:, None] * (4 * q[None, :] + p), 1024)
        c, s = c.astype(np.float32), s.astype(np.float32)
        third.append(np.concatenate([c, s], 1))
    n1 = np.arange(1024)
    c, s = phases(n1[:, None] * np.arange(128)[None, :], NSAMP)
    back = np.stack([c, s]).astype(np.float32)
    c, s = phases(n1[:, None] * 128 * np.arange(128)[None, :], NSAMP)
    shift = np.stack([c, s]).astype(np.float32)
    last = []
    for p in range(4):
        c, s = phases((4 * q[:, None] + p) * q[None, :], 1024)
        last.append(np.stack([c, s]).astype(np.float32))
    return dict(
        first=first,
        second=second,
        third=np.stack(third).astype(jnp.bfloat16),
        back=back,
        shift=shift,
        last=np.stack(last).astype(jnp.bfloat16),
    )


def dot(a, b):
    return jnp.dot(a, b, preferred_element_type=F32)


def dot_nt(a, b):
    return lax.dot_general(a, b, (((1,), (1,)), ((), ())), preferred_element_type=F32)


def place():
    t = lax.axis_index("tmpl")
    return t // 4, (t // 2) % 2, t % 2


def gate_kernel(
    strain_ref, start_any, span_any, assign_any, bank_any, asd_any, back_any, shift_any,
    out_ref, weight_ref, twist_ref, *rest
):
    pick_refs, rest = rest[:8], rest[8:]
    strain, bank_ref, start_ref, span_ref, assign_ref, asd_ref, back_ref, shift_ref, sems = rest
    x, z, core = place()
    copies = [
        pltpu.make_async_copy(start_any, start_ref, sems.at[0]),
        pltpu.make_async_copy(span_any, span_ref, sems.at[1]),
        pltpu.make_async_copy(strain_ref.at[core], strain, sems.at[2]),
        pltpu.make_async_copy(assign_any, assign_ref, sems.at[3]),
        pltpu.make_async_copy(bank_any, bank_ref, sems.at[4]),
        pltpu.make_async_copy(asd_any, asd_ref, sems.at[5]),
        pltpu.make_async_copy(back_any, back_ref, sems.at[6]),
        pltpu.make_async_copy(shift_any, shift_ref, sems.at[7]),
    ]
    for copy in copies:
        copy.start()
    row = lax.broadcasted_iota(jnp.int32, (128, 128), 0)
    lane = lax.broadcasted_iota(jnp.int32, (128, 128), 1)
    order = jnp.where(lane == row % 32 * 4 + row // 32, 1.0, 0.0).astype(BF)
    pick = jnp.where(row == lane % 32 * 4 + lane // 32, 1.0, 0.0).astype(BF)
    for copy in copies[:3]:
        copy.wait()
    blocks = []
    for dest in range(8):
        value = strain[:, 128 * dest : 128 * dest + 128]
        sample = row * 1024 + (lane + 128 * dest)
        for g in range(2):
            first = start_ref[core, 0, g]
            inside = (sample >= first) & (sample < first + span_ref[core, 0, g])
            value = jnp.where(inside, 0.0, value)
        blocks.append(value.astype(BF))
    picked = dot(jnp.concatenate(blocks, axis=0), pick).astype(BF)
    wide = jnp.concatenate([picked[128 * dest : 128 * dest + 128] for dest in range(8)], axis=1)
    ordered = dot(order, wide).astype(BF)
    for dest in range(8):
        out_ref[dest] = ordered[:, 128 * dest : 128 * dest + 128]

    for copy in copies[3:5]:
        copy.wait()
    for i in range(16):
        (rz, rx), rc = OFFSETS[i // 2], i % 2
        dest = ((x + rx) % 4) * 4 + (z + rz) % 2 * 2 + (core + rc) % 2
        for slot in range(2):
            chosen = assign_ref[2 * dest + slot]
            for part in range(2):
                for p in range(4):
                    value = bank_ref[part, chosen, pl.ds(p, 16, stride=4), :].astype(BF)
                    pick_refs[i // 2][rc, slot, part, p] = value

    for copy in copies[5:]:
        copy.wait()
    for p in range(4):
        asd = asd_ref[pl.ds(p, 256, stride=4), :]
        weight_ref[p] = 1.0 / (asd * asd)
    own = lane == lax.axis_index("seg")
    for i in range(8):
        rows = slice(128 * i, 128 * i + 128)
        shift = [jnp.sum(jnp.where(own, shift_ref[part, rows, :], 0.0), axis=1, keepdims=True) for part in range(2)]
        re, im = back_ref[0, rows, :], back_ref[1, rows, :]
        twist_ref[0, rows, :] = re * shift[0] - im * shift[1]
        twist_ref[1, rows, :] = re * shift[1] + im * shift[0]


def pack_kernel(*refs):
    piece_refs, _, out_ref, sems = refs[:4], *refs[4:]
    copies = [pltpu.make_async_copy(piece_refs[i].at[1], out_ref.at[i], sems.at[i]) for i in range(4)]
    for copy in copies:
        copy.start()
    for copy in copies:
        copy.wait()


def four_way(sign, parts):
    (ar, ai), (br, bi), (cr, ci), (dr, di) = parts
    sr, si = ar + cr, ai + ci
    tr, ti = ar - cr, ai - ci
    ur, ui = br + dr, bi + di
    vr, vi = br - dr, bi - di
    if sign > 0:
        wr, wi = -vi, vr
    else:
        wr, wi = vi, -vr
    return ((sr + ur, si + ui), (tr + wr, ti + wi), (sr - ur, si - ui), (tr - wr, ti - wi))


def first_kernel(cols_ref, table_ref, *refs):
    out_ref, token_ref, z_ref = refs[-3:]
    token_ref[...] = jnp.zeros_like(token_ref)
    turn_ref = table_ref.at[256:368].reshape(2, 56, 1024)
    turned = jnp.concatenate([cols_ref[:, 32 * r : 32 * r + 32, :].reshape(256, 128).T for r in range(4)], axis=0)
    z_ref[...] = dot(turned, table_ref[:256, :512].astype(BF)) + dot(turned, table_ref[:256, 512:].astype(BF))
    seg = 32 + lax.axis_index("seg")
    seg_re, seg_im = turn_ref[0, pl.ds(seg, 1), :], turn_ref[1, pl.ds(seg, 1), :]
    for r1 in range(4):
        low_re, low_im = turn_ref[0, 40 + r1 : 41 + r1, :], turn_ref[1, 40 + r1 : 41 + r1, :]
        base_re = low_re * seg_re - low_im * seg_im
        base_im = low_re * seg_im + low_im * seg_re
        for i in range(2):
            at = slice(16 * i, 16 * i + 16)
            rows = slice(32 * r1 + 16 * i, 32 * r1 + 16 * i + 16)
            fr, fi = turn_ref[0, at, :], turn_ref[1, at, :]
            tr = fr * base_re - fi * base_im
            ti = fr * base_im + fi * base_re
            sums = []
            for r in range(4):
                here = slice(128 * r + rows.start, 128 * r + rows.stop)
                re, im = z_ref[here, :256], z_ref[here, 256:]
                if r > 0:
                    pr, pi = turn_ref[0, 48 + r : 49 + r, :256], turn_ref[1, 48 + r : 49 + r, :256]
                    re, im = re * pr - im * pi, re * pi + im * pr
                sums.append((re, im))
            outs = four_way(-1, sums)
            for k, (re, im) in enumerate(outs):
                wr, wi = tr[:, 256 * k : 256 * k + 256], ti[:, 256 * k : 256 * k + 256]
                done = ((re * wr - im * wi).astype(BF), (re * wi + im * wr).astype(BF))
                for half in range(2):
                    for part in range(2):
                        out_ref[2 * k + half, part, r1, at] = done[part][:, 128 * half : 128 * half + 128]


def second_kernel(own_ref, table_ref, after_ref, also_ref, spec_ref, z_ref):
    del after_ref, also_ref
    hi, lo = table_ref[:, :512].astype(BF), table_ref[:, 512:1024].astype(BF)
    for r in range(4):
        re = own_ref[:, 0, r].reshape(256, 128)
        im = own_ref[:, 1, r].reshape(256, 128)
        right = jnp.concatenate([jnp.concatenate([re, im], axis=1), jnp.concatenate([im, -re], axis=1)], axis=0)
        z_ref[r] = dot(hi, right) + dot(lo, right)
    for i in range(8):
        rows = slice(32 * i, 32 * i + 32)
        sums = [(z_ref[0, rows, :128], z_ref[0, rows, 128:])]
        for r in range(1, 4):
            at = 1024 + 2 * r
            pr, pi = table_ref[rows, at : at + 1], table_ref[rows, at + 1 : at + 2]
            re, im = z_ref[r, rows, :128], z_ref[r, rows, 128:]
            sums.append((re * pr - im * pi, re * pi + im * pr))
        for k, parts in enumerate(four_way(-1, sums)):
            for part in range(2):
                spec_ref[part, 256 * k + 32 * i : 256 * k + 32 * i + 32, :] = parts[part]


def assemble_kernel(*refs):
    piece_refs, cross_refs, bank, sems = refs[:8], refs[8:10], *refs[10:]
    x, z, core = place()
    copies = []
    for i, (rz, rx) in enumerate(OFFSETS):
        for rc in range(2):
            src = piece_refs[i].at[0] if rc == 0 else cross_refs[i // 4].at[i % 4]
            origin = ((x + 4 - rx) % 4) * 4 + (z + rz) % 2 * 2 + (core + rc) % 2
            copies.append(pltpu.make_async_copy(src, bank.at[origin], sems.at[len(copies)]))
    for copy in copies:
        copy.start()
    for copy in copies:
        copy.wait()


def filter_segment(spec, weight_ref, third_ref, twist, bank, out_ref, first_row, v_ref, norms):
    for p in range(4):
        weight = weight_ref[p]
        sr = spec[0, pl.ds(p, 256, stride=4), :] * weight
        si = spec[1, pl.ds(p, 256, stride=4), :] * weight
        lanes_re, lanes_im = [], []
        for slot in range(2):
            hr = bank[:, slot, 0, p].reshape(256, 128).astype(F32)
            hi = bank[:, slot, 1, p].reshape(256, 128).astype(F32)
            if norms is not None:
                power = (hr * hr + hi * hi) * weight
                norms[slot] = norms[slot] + power.reshape(32, 8, 128).sum(axis=0)
            lanes_re.append((sr * hr + si * hi).astype(BF))
            lanes_im.append((si * hr - sr * hi).astype(BF))
        re, im = jnp.concatenate(lanes_re, axis=1), jnp.concatenate(lanes_im, axis=1)
        v_ref[p, 0] = dot(third_ref[p], jnp.concatenate([re, -im], axis=0))
        v_ref[p, 1] = dot(third_ref[p], jnp.concatenate([im, re], axis=0))
    for i in range(8):
        rows = slice(32 * i, 32 * i + 32)
        half, inside = i // 4, (i % 4) * 32
        for slot in range(2):
            cols = slice(128 * slot, 128 * slot + 128)
            outs = four_way(1, [(v_ref[p, 0, rows, cols], v_ref[p, 1, rows, cols]) for p in range(4)])
            for k, (re, im) in enumerate(outs):
                wr = twist[0, 256 * k + 32 * i : 256 * k + 32 * i + 32, :]
                wi = twist[1, 256 * k + 32 * i : 256 * k + 32 * i + 32, :]
                at = first_row + slot * 256 + inside
                out_ref[2 * k + half, at : at + 32, :] = (re * wr - im * wi).astype(BF)
                out_ref[2 * k + half, at + 128 : at + 160, :] = (re * wi + im * wr).astype(BF)


def own_kernel(spec, weight_ref, third_ref, twist, bank, out_ref, v_ref):
    norms = [jnp.zeros((8, 128), F32), jnp.zeros((8, 128), F32)]
    filter_segment(spec, weight_ref, third_ref, twist, bank, out_ref, 0, v_ref, norms)
    row = lax.broadcasted_iota(jnp.int32, (16, 128), 0)
    tail = jnp.zeros((16, 128), F32)
    for slot in range(2):
        left = jnp.broadcast_to(norms[slot].sum(axis=0, keepdims=True), (16, 128))
        for piece in range(3):
            rounded = left.astype(BF).astype(F32)
            tail = jnp.where(row == 3 * slot + piece, rounded, tail)
            left = left - rounded
    for dest in range(8):
        out_ref[dest, 512:528, :] = tail.astype(BF)


def other_kernel(spec, weight_ref, third_ref, twist, bank, half_ref, out_ref, v_ref):
    out_ref[:, :528, :] = half_ref[...]
    filter_segment(spec, weight_ref, third_ref, twist, bank, out_ref, 528, v_ref, None)


def last_kernel(in_ref, table_ref, out_any, out_ref, sems):
    total = jnp.zeros((16, 128), F32)
    for s in range(8):
        total = total + in_ref[s, 512:528, :].astype(F32)
    row = lax.broadcasted_iota(jnp.int32, (16, 128), 0)
    scales = []
    for slot in range(2):
        mine = (row >= 3 * slot) & (row < 3 * slot + 3)
        sigma2 = jnp.sum(jnp.where(mine, total, 0.0), axis=(0, 1), keepdims=True)
        scales.append(1.0 / jnp.sqrt(NSAMP * sigma2))
    _, _, core = place()
    copies = []
    for pair in range(4):
        other, slot = pair // 2, pair % 2
        seg = (core + other) % 2
        at = 528 * other + 256 * slot
        parts = []
        for r in range(4):
            both = jnp.concatenate([in_ref[2 * r, at : at + 256, :], in_ref[2 * r + 1, at : at + 256, :]], axis=1)
            both = both.astype(F32)
            parts.append((both[:128], both[128:]))
        outs = four_way(1, parts)
        for p, (re, im) in enumerate(outs):
            right = jnp.concatenate([re, im], axis=0).astype(BF)
            cos = dot_nt(table_ref[p, 0], right)
            sin = dot_nt(table_ref[p, 1], right)
            sr = cos[:, :128] - sin[:, 128:]
            si = sin[:, :128] + cos[:, 128:]
            out_ref[pair, pl.ds(p, 256, stride=4), :] = jnp.sqrt(sr * sr + si * si) * scales[slot]
        copies.append(pltpu.make_async_copy(out_ref.at[pair], out_any.at[seg, slot], sems.at[pair]))
        copies[pair].start()
    for copy in copies:
        copy.wait()


def call(kernel, ins, outs, specs, flops, moved, scratch=(), limit=16, space=VMEM):
    return pl.pallas_call(
        kernel,
        out_shape=outs,
        in_specs=specs,
        out_specs=space if isinstance(space, tuple) else jax.tree.map(lambda _: space, outs),
        scratch_shapes=list(scratch),
        compiler_params=pltpu.CompilerParams(vmem_limit_bytes=limit * MIB),
        cost_estimate=pl.CostEstimate(flops=flops, bytes_accessed=moved, transcendentals=0),
    )(*ins)


def shape(*dims, dtype=BF):
    return jax.ShapeDtypeStruct(dims, dtype)


def per_device(strain, gate_start, gate_span, asd, bank, assign):
    const = {name: jnp.asarray(value) for name, value in tables().items()}
    swap_core = [(i, i ^ 1) for i in range(16)]

    blk = (2, 2, 4, 16, 128)
    gated, weight, twist, *picked = call(
        gate_kernel, (strain, gate_start, gate_span, assign, bank, asd, const["back"], const["shift"]),
        (
            shape(8, 128, 128), shape(4, 256, 128, dtype=F32), shape(2, 1024, 128, dtype=F32),
            *[shape(2, *blk)] * 8,
        ),
        [ANY] * 8, 10**8, 4 * MIB,
        [
            pltpu.VMEM((128, 1024), F32), pltpu.VMEM((2, 32, 64, 128), F32), pltpu.SMEM((2, 1, 2), jnp.int32),
            pltpu.SMEM((2, 1, 2), jnp.int32), pltpu.SMEM((32,), jnp.int32), pltpu.VMEM((1024, 128), F32),
            pltpu.VMEM((2, 1024, 128), F32), pltpu.VMEM((2, 1024, 128), F32), pltpu.SemaphoreType.DMA((8,)),
        ],
        limit=63,
    )
    columns = lax.all_to_all(gated, "seg", 0, 0)

    pieces = picked[:1]
    for (rz, rx), send in zip(OFFSETS[1:], picked[1:]):
        hop = [(i, (i // 4 + rx) % 4 * 4 + i % 4 ^ 2 * rz) for i in range(16)]
        pieces.append(lax.ppermute(send, "tmpl", hop))
    turned, token = call(
        first_kernel, (columns, const["first"], *pieces[1:4]), (shape(8, 2, 4, 32, 128), shape(8, 128, dtype=F32)),
        [VMEM] * 2 + [ANY] * 3, 3 * 10**8, 4 * MIB, [pltpu.VMEM((512, 512), F32)],
    )
    crosses = [
        call(
            pack_kernel, (*pieces[i : i + 4], token), shape(4, *blk), [ANY] * 5, 1, MIB,
            [pltpu.SemaphoreType.DMA((4,))], limit=8, space=ANY,
        )
        for i in (0, 4)
    ]
    crossed = [lax.ppermute(cross, "tmpl", swap_core) for cross in crosses]
    ordered = call(
        assemble_kernel, (*pieces, *crossed), shape(16, *blk), [ANY] * 10, 1, 10 * MIB,
        [pltpu.SemaphoreType.DMA((16,))], limit=8,
    )
    own = lax.all_to_all(turned, "seg", 0, 0)
    spec = call(
        second_kernel, (own, const["second"], *crossed), shape(2, 1024, 128, dtype=F32),
        [VMEM] * 2 + [ANY] * 2, 1, 1, [pltpu.VMEM((4, 256, 256), F32)],
    )
    other_spec = lax.ppermute(spec, "tmpl", swap_core)
    half = call(
        own_kernel,
        (spec, weight, const["third"], twist, ordered),
        shape(8, 528, 128), [VMEM] * 5, 2 * 10**9, 10 * MIB, [pltpu.VMEM((4, 2, 256, 256), F32)],
    )
    inner = call(
        other_kernel,
        (other_spec, weight, const["third"], twist, ordered, half),
        shape(8, 1040, 128), [VMEM] * 6, 2 * 10**9, 10 * MIB, [pltpu.VMEM((4, 2, 256, 256), F32)],
    )
    series = lax.all_to_all(inner, "seg", 0, 0)
    return call(
        last_kernel, (series, const["last"]), shape(2, 2, 1024, 128, dtype=F32), [VMEM] * 2, 3 * 10**9, 6 * MIB,
        [pltpu.VMEM((4, 1024, 128), F32), pltpu.SemaphoreType.DMA((4,))], space=ANY,
    )


def solution(mesh):
    placed = (
        P(None, "seg", None),
        P(None, "seg", None),
        P(None, "seg", None),
        P(None, "seg"),
        P(None, None, "tmpl", "seg"),
        P(),
    )
    return jax.shard_map(
        per_device,
        mesh=mesh,
        in_specs=placed,
        out_specs=P(None, "tmpl", None, "seg"),
        check_vma=False,
    )
```
